32 devices in a mesh: ka: 16 (over z, y, x), ta: 2 (over core).
Axes of the slice: x: 2, y: 2, z: 4, core: 2. Of those that a mesh axis runs over, the one named last changes fastest.
Arguments:
- sigma_history: bfloat16 [32, 1024, 256], P('ka', 'ta'), may hold values from -6 to 6
- time_basis: bfloat16 [1024, 64], P('ta'), may hold values from -0.75 to 0.75
- history_coef: bfloat16 [32, 128, 256], P('ka', 'ta'), may hold values from -6 to 6
- green_now: float32 [32, 256], P('ka'), may hold values from -6 to 6
- hamilton: float32 [32, 256], P('ka'), may hold values from -1.5 to 1.5
- panel_block: bfloat16 [32, 512, 512], P('ka', 'ta'), may hold values from -7 to 7
- panel_lengths: int32 [2], P('ta'), may hold values from 1 to 16, 24 in all
- owners: int32 [32, 1], P('ka'), may hold values from 0 to 3
- sketch: bfloat16 [4, 512, 64], P(None, 'ka'), may hold values from -6 to 6
Outputs:
- green_next: float32 [32, 256], P('ka')
- ortho_factor: float32 [32, 512, 64], P('ka', 'ta')
- coef_factor: float32 [32, 64, 512], P('ka', None, 'ta')
The draws below stay inside these ranges and needn't reach their ends.
Inputs may be any that keep to these rules, and one draw needn't show every extreme that they name: `owners`: every compressor rank serves some k-point. `panel_lengths`: they sum to 24; the largest is 16.
All inputs are finite; a program needn't handle non-finite values. No bound on the sum of `panel_lengths` on one device may be relied on, other than what follows from the above.
Results may differ from the reference program's by a relative error of at most 0.0095.
Values may be sent and summed in bfloat16 or wider, within the bound.
A program may use at most 64 MiB of HBM per device.

```python
import math
import jax
import jax.numpy as jnp
import numpy as np
from jax import lax

NO = 16
OO = 256
R = 64
HIST_DEV = 512
PROW_DEV = 16
NCMP = 4
KPTS = 32
HORIZON = 1024
NTB = 2
RB = 128
PROWS = 512
PCOLS = 512
TOTAL = 24
N_TA = 2


def draw_panel_block(key, part):
    shape = (KPTS, PROWS, PCOLS)
    values = jax.random.normal(jax.random.fold_in(key, 12), shape, jnp.float32)
    return jnp.clip(values, -6.0, 6.0).astype(jnp.bfloat16)


def draw_sketch(key, part):
    shape = (NCMP, PCOLS, R)
    values = jax.random.normal(jax.random.fold_in(key, 22), shape, jnp.float32)
    return jnp.clip(values, -6.0, 6.0).astype(jnp.bfloat16)


def block_levels(key, dims, cuts, smallest, top_value):
    loudness, own = 1.0, jax.random.fold_in(key, 6)
    for dim, shards_of in cuts:
        draws = jnp.exp(jax.random.uniform(jax.random.fold_in(own, dim), (shards_of,), jnp.float32, smallest / len(cuts), top_value / len(cuts)))
        loudness = loudness * jnp.repeat(draws, dims[dim] // shards_of).reshape([-1 if axis == dim else 1 for axis in range(len(dims))])
    return loudness


def picks_of(stream_key, rows, count, top, lift):
    ranking = jax.random.permutation(jax.random.fold_in(stream_key, 1), count)
    boost = ranking
    for power in range(3):
        boost = boost * boost // count
    boost = boost * lift // count
    tickets = jax.random.randint(jax.random.fold_in(stream_key, 2), (rows, count), 0, 4096) + boost
    sure = jax.random.permutation(jax.random.fold_in(stream_key, 3), rows)[jnp.arange(count) % rows]
    tickets = jnp.where(jnp.arange(rows)[:, None] == sure[None, :], 1 << 14, tickets)
    score = tickets * count + jnp.arange(count)
    return lax.top_k(score.astype(jnp.int32), top)[1].astype(jnp.int32)


def length_profile(amount, total, limit, skew):
    weights = [(1 << 20) // math.isqrt(rank ** skew) + 1 for rank in range(2, amount + 1)]
    surplus, counts = total - limit - (amount - 1), [1] * (amount - 1)
    while surplus > 0:
        movable = [i for i in range(amount - 1) if counts[i] < limit]
        mass, left = sum([weights[i] for i in movable]), surplus
        for i in movable:
            more = min(limit - counts[i], max(1, left * weights[i] // mass), surplus)
            counts[i] = counts[i] + more
            surplus = surplus - more
    return np.array([limit] + counts)


def uneven(stream_key, number_of, total, bound, lean):
    if number_of == 2:
        one = jax.random.randint(stream_key, (), max(1, total - bound), min(bound, total - 1) + 1)
        return jnp.stack([one, total - one])
    lengths = jnp.asarray(length_profile(number_of, total, bound, lean), jnp.int32)
    couples = (number_of - 1) // 2
    donor, sink = lengths[1:1 + 2 * couples:2], lengths[2:2 + 2 * couples:2]
    room = jnp.minimum(donor - 1, bound - sink)
    passed = jax.random.randint(jax.random.fold_in(stream_key, 1), (couples,), 0, 1 << 20) % (room + 1)
    lengths = lengths.at[1:1 + 2 * couples:2].set(donor - passed).at[2:2 + 2 * couples:2].set(sink + passed)
    return lengths[jax.random.permutation(jax.random.fold_in(stream_key, 2), number_of)]


def scatter_about(stream_key, shape, width, most, pieces=(), kind=jnp.bfloat16):
    drawn = jax.random.normal(stream_key, shape, jnp.float32) * width
    if len(pieces) > 0:
        drawn = block_levels(stream_key, shape, pieces, -0.22, 0.18) * drawn
    return jnp.clip(drawn, min=-most, max=most).astype(kind)


def setup_inputs(seed: int = 0) -> dict:
    splits = jax.random.split(jax.random.key(seed), 10)
    return {
        "sigma_history": scatter_about(splits[0], (KPTS, HORIZON, OO), 1.0, 6.0, ((0, 16), (1, 2))),
        "time_basis": scatter_about(splits[1], (HORIZON, R), R ** -0.5, 0.75, ((0, 2),)),
        "history_coef": scatter_about(splits[2], (KPTS, RB, OO), 1.0, 6.0, ((0, 16), (1, 2))),
        "green_now": scatter_about(splits[3], (KPTS, OO), 1.0, 6.0, ((0, 16),), jnp.float32),
        "hamilton": scatter_about(splits[4], (KPTS, OO), 0.25, 1.5, ((0, 16),), jnp.float32),
        "panel_block": draw_panel_block(jax.random.fold_in(splits[9], 71), 0),
        "panel_lengths": uneven(splits[6], NTB, TOTAL, PROW_DEV, 2).astype(jnp.int32),
        "owners": picks_of(splits[7], KPTS, NCMP, 1, 4096),
        "sketch": draw_sketch(jax.random.fold_in(splits[9], 71), 0),
    }


step_size = 0.25

def reference(sigma_history, time_basis, history_coef, green_now, hamilton, panel_block, panel_lengths, owners, sketch):
    high = lax.Precision.HIGHEST

    def block_term(carry, block_index):
        sigma_block = lax.dynamic_slice_in_dim(sigma_history, block_index * HIST_DEV, HIST_DEV, 1).astype(jnp.float32)
        basis_block = lax.dynamic_slice_in_dim(time_basis, block_index * HIST_DEV, HIST_DEV, 0).astype(jnp.float32)
        coef_block = lax.dynamic_slice_in_dim(history_coef, block_index * R, R, 1).astype(jnp.float32)
        summed = jnp.einsum('jr,kjo->kro', basis_block, sigma_block, precision=high).reshape(KPTS, R, NO, NO)
        coef_block = coef_block.reshape(KPTS, R, NO, NO)
        return (carry + jnp.einsum('krac,krcd->kad', summed, coef_block, precision=high), None)
    blocks = jnp.arange(N_TA, dtype=jnp.int32)
    total_term, unused = lax.scan(block_term, jnp.zeros((KPTS, NO, NO), jnp.float32), blocks)
    integral = total_term / jnp.sqrt(jnp.float32(NO * HORIZON))
    green = green_now.reshape(KPTS, NO, NO)
    hmat = hamilton.reshape(KPTS, NO, NO)
    for repeat in range(2):
        left_prod = jnp.einsum('kac,kcd->kad', hmat, green, precision=high)
        right_prod = jnp.einsum('kac,kcd->kad', green, hmat, precision=high)
        green = green + step_size * (left_prod - right_prod + integral)
    green_next = green.reshape(KPTS, NO * NO)
    starts = jnp.cumsum(panel_lengths) - panel_lengths
    slot_index = jnp.arange(PROW_DEV, dtype=jnp.int32)
    row_time = starts[:, None] + slot_index[None, :]
    row_live = slot_index[None, :] < panel_lengths[:, None]
    col_time = jnp.arange(PCOLS, dtype=jnp.int32) // NO - PROW_DEV // 2
    keep = row_live[:, :, None, None] & (col_time[None, None, None, :] <= row_time[:, :, None, None])
    keep = jnp.broadcast_to(keep, (N_TA, PROW_DEV, NO, PCOLS)).reshape(PROWS, PCOLS)
    masked = jnp.where(keep[None], panel_block, jnp.zeros_like(panel_block))
    omega = jnp.take(sketch, owners[:, 0], axis=0)
    sketched = jnp.einsum('krx,kxq->krq', masked.astype(jnp.float32), omega.astype(jnp.float32), precision=high)
    gram = jnp.einsum('krq,krp->kqp', sketched, sketched, precision=high)
    lower = jnp.linalg.cholesky(gram)
    ortho = lax.linalg.triangular_solve(lower, sketched, left_side=False, lower=True, transpose_a=True)
    rounded = lax.optimization_barrier(ortho.astype(jnp.bfloat16)).astype(jnp.float32)
    rounded_blocks = rounded.reshape(KPTS, N_TA, PROW_DEV * NO, R)
    masked_blocks = masked.astype(jnp.float32).reshape(KPTS, N_TA, PROW_DEV * NO, PCOLS)
    partial_terms = jnp.einsum('kbrq,kbrc->kbqc', rounded_blocks, masked_blocks, precision=high)
    partial_terms = lax.optimization_barrier(partial_terms.astype(jnp.bfloat16)).astype(jnp.float32)
    coef_factor = lax.optimization_barrier(jnp.sum(partial_terms, axis=1))
    return (green_next, ortho, coef_factor)
```

```python
import functools
import math

import jax
import jax.numpy as jnp
from jax import lax
from jax.experimental import pallas as pl
from jax.experimental.pallas import tpu as pltpu
from jax.sharding import PartitionSpec as P

MESH = pl.DeviceIdType.MESH
HIGH = lax.Precision.HIGHEST
F32 = jnp.float32
BF16 = jnp.bfloat16
STEP = 0.25
GROUP = 4


def iota(shape, dim):
    return lax.broadcasted_iota(jnp.int32, shape, dim)


def dot(a, b, da=1, db=0, precision=None):
    return lax.dot_general(
        a, b, (((da,), (db,)), ((), ())), precision=precision, preferred_element_type=F32
    )


def eliminate(mats, offsets, rank):
    count = rank // 8
    full = (8, mats[0].shape[1])
    sub = iota(full, 0)
    tiles = [[m[8 * i : 8 * i + 8] for i in range(count)] for m in mats]
    pivots = [[None] * count for _ in mats]
    for j in range(count):
        cols = [
            [
                [
                    jnp.broadcast_to(t[i][:, o + 8 * j + a : o + 8 * j + a + 1], full)
                    for a in range(8)
                ]
                for i in range(j, count)
            ]
            for t, o in zip(tiles, offsets)
        ]
        for n, t in enumerate(tiles):
            pivots[n][j] = jnp.ones(full, F32)
        for a in range(8):
            for n, t in enumerate(tiles):
                c = cols[n]
                pivot = jnp.broadcast_to(c[0][a][a : a + 1], full)
                inverse = 1.0 / pivot
                pivots[n][j] = jnp.where(sub == a, pivot, pivots[n][j])
                row = jnp.broadcast_to(t[j][a : a + 1], full)
                heads = [jnp.broadcast_to(c[0][b][a : a + 1], full) for b in range(a + 1, 8)]
                for i in range(j, count):
                    if i == j:
                        if a == 7:
                            continue
                        factor = jnp.where(sub > a, c[0][a] * inverse, 0.0)
                    else:
                        factor = c[i - j][a] * inverse
                    for b in range(a + 1, 8):
                        c[i - j][b] = c[i - j][b] - factor * heads[b - a - 1]
                    t[i] = t[i] - factor * row
    return [
        jnp.concatenate([x * lax.rsqrt(p) for x, p in zip(t, pv)], axis=0)
        for t, pv in zip(tiles, pivots)
    ]


def kernel(
    n_ka,
    n_ta,
    length_ref,
    start_ref,
    owner_ref,
    green_ref,
    ham_ref,
    sigma_hbm,
    basis_hbm,
    hist_hbm,
    panel_hbm,
    sketch_hbm,
    green_out,
    ortho_out,
    coef_out,
    sigma_ref,
    basis_ref,
    hist_ref,
    panel_ref,
    sketch_ref,
    packed,
    gathered,
    masked,
    part,
    parts,
    right,
    rights,
    local_sem,
    send1,
    recv1,
    send2,
    recv2,
    send3,
    recv3,
    send4,
    recv4,
):
    ka, ta = lax.axis_index("ka"), lax.axis_index("ta")
    k_local, rows, cols = panel_ref.shape
    rank = sketch_ref.shape[2]
    depth = sketch_ref.shape[1]
    ranks = sketch_ref.shape[0]
    share = ranks // 2 // n_ta
    oo = sigma_ref.shape[2]
    no = math.isqrt(oo)
    width = 2 * rank

    loads = [
        pltpu.make_async_copy(src, dst, local_sem.at[i])
        for i, (src, dst) in enumerate(
            [
                (sketch_hbm, sketch_ref),
                (panel_hbm, panel_ref),
                (basis_hbm, basis_ref),
                (sigma_hbm, sigma_ref),
                (hist_hbm, hist_ref),
            ]
        )
    ]
    for load in loads:
        load.start()

    barrier = pltpu.get_barrier_semaphore()
    for off in range(1, n_ka):
        pl.semaphore_signal(
            barrier, inc=1, device_id=(lax.rem(ka + off, n_ka), ta), device_id_type=MESH
        )
    for off in range(1, n_ta):
        pl.semaphore_signal(
            barrier, inc=1, device_id=(ka, lax.rem(ta + off, n_ta)), device_id_type=MESH
        )
    loads[0].wait()
    for pair in range(ranks // 2):
        packed[pair // share, pair % share] = jnp.concatenate(
            [sketch_ref[2 * pair], sketch_ref[2 * pair + 1]], axis=1
        )
    gathered[ta, ka] = packed[ta]
    pl.semaphore_wait(barrier, n_ka - 1 + n_ta - 1)

    first = []
    for off in range(n_ka - 1, 0, -1):
        to = lax.rem(ka + off, n_ka)
        copy = pltpu.make_async_remote_copy(
            src_ref=packed.at[ta],
            dst_ref=gathered.at[ta, ka],
            send_sem=send1.at[off],
            recv_sem=recv1.at[ka],
            device_id=(to, ta),
            device_id_type=MESH,
        )
        copy.start()
        first.append(copy)

    row = iota((rows, cols), 0)
    col = iota((rows, cols), 1)
    slot_row = lax.div(row, no) * no
    slots = rows // no
    keep = (col < (start_ref[0] + slots // 2 + 1) * no + slot_row) & (row < length_ref[0] * no)
    unit = jnp.where(keep, 1.0, 0.0).astype(BF16)
    loads[1].wait()
    for k in range(k_local):
        masked[k] = panel_ref[k] * unit

    gather_a = jnp.where(lax.div(iota((no, oo), 1), no) == iota((no, oo), 0), 1.0, 0.0)
    gather_d = jnp.where(
        lax.rem(iota((oo, no), 0), no) == iota((oo, no), 1), 1.0, 0.0
    )
    diag = lax.rem(iota((oo, oo), 0), no) == lax.div(iota((oo, oo), 1), no)
    for load in loads[2:]:
        load.wait()
    basis = basis_ref[...]
    for k in range(k_local):
        summed = dot(basis, sigma_ref[k])
        outer = dot(summed, hist_ref[k].astype(F32), 0, 0, HIGH)
        outer = jnp.where(diag, outer, 0.0)
        lane = iota((oo, width), 1) - (k % 2) * rank
        place = jnp.where(lax.rem(iota((oo, width), 0), no) == lane, 1.0, 0.0)
        piece = dot(dot(gather_a, outer, 1, 0, HIGH), place, 1, 0, HIGH)
        if k % 2 == 0:
            part[k // 2, rank:] = piece
        else:
            part[k // 2, rank:] = part[k // 2, rank:] + piece

    groups = n_ka // GROUP
    second = []
    mine = lax.div(ka, GROUP)
    for g in range(groups):
        group = lax.rem(mine + g, groups)
        for i in range(GROUP):
            source = group * GROUP + i

            @pl.when(source != ka)
            def _():
                pltpu.make_async_remote_copy(
                    src_ref=packed.at[ta],
                    dst_ref=gathered.at[ta, source],
                    send_sem=send1.at[0],
                    recv_sem=recv1.at[source],
                    device_id=(ka, lax.rem(ta + 1, n_ta)),
                    device_id_type=MESH,
                ).wait_recv()

        for off in range(1, n_ta):
            piece = gathered.at[ta, pl.ds(group * GROUP, GROUP)]
            copy = pltpu.make_async_remote_copy(
                src_ref=piece,
                dst_ref=piece,
                send_sem=send2.at[off, g],
                recv_sem=recv2.at[ta, group],
                device_id=(ka, lax.rem(ta + off, n_ta)),
                device_id_type=MESH,
            )
            copy.start()
            second.append(copy)
    for copy in first:
        copy.wait_send()
    for off in range(1, n_ta):
        source = lax.rem(ta + off, n_ta)
        for g in range(groups):
            piece = gathered.at[source, pl.ds(g * GROUP, GROUP)]
            pltpu.make_async_remote_copy(
                src_ref=piece,
                dst_ref=piece,
                send_sem=send2.at[off, g],
                recv_sem=recv2.at[source, g],
                device_id=(ka, source),
                device_id_type=MESH,
            ).wait_recv()

    sketched = []
    grams = []
    for k in range(k_local):
        owner = owner_ref[k]
        pair = lax.div(owner, 2)
        omega = gathered[lax.div(pair, share), :, lax.rem(pair, share)]
        both = dot(omega.reshape(n_ka * depth, width), masked[k], 0, 1)
        value = jnp.where(lax.rem(owner, 2) == 0, both[:rank], both[rank:])
        sketched.append(value)
        grams.append(dot(value, value, 1, 1, HIGH))
    for p in range(k_local // 2):
        part[p, :rank] = jnp.concatenate([grams[2 * p], grams[2 * p + 1]], axis=1)

    third = []
    for off in range(1, n_ta):
        copy = pltpu.make_async_remote_copy(
            src_ref=part,
            dst_ref=parts.at[ta],
            send_sem=send3.at[off],
            recv_sem=recv3.at[ta],
            device_id=(ka, lax.rem(ta + off, n_ta)),
            device_id_type=MESH,
        )
        copy.start()
        third.append(copy)
    for copy in second:
        copy.wait_send()
    for off in range(1, n_ta):
        source = lax.rem(ta + off, n_ta)
        pltpu.make_async_remote_copy(
            src_ref=part,
            dst_ref=parts.at[source],
            send_sem=send3.at[off],
            recv_sem=recv3.at[source],
            device_id=(ka, source),
            device_id_type=MESH,
        ).wait_recv()
    parts[ta] = part[...]
    total = parts[0]
    for b in range(1, n_ta):
        total = total + parts[b]

    lane = iota((rank, width), 1)
    line = iota((rank, width), 0)
    integrals = []
    for p in range(k_local // 2):
        gram = total[p, :rank]
        left = jnp.where(lane < rank, gram, jnp.where(lane == line + rank, 1.0, 0.0))
        other = jnp.where(lane >= rank, gram, jnp.where(lane == line, 1.0, 0.0))
        low, high = eliminate([left, other], [0, rank], rank)
        low = jnp.where(lane >= rank, low, 0.0)
        high = jnp.where(lane < rank, high, 0.0)
        empty = jnp.zeros((rank, rows), F32)
        low_st = jnp.concatenate([empty, sketched[2 * p]], axis=0)
        high_st = jnp.concatenate([sketched[2 * p + 1], empty], axis=0)
        ortho_out[2 * p] = dot(low, low_st, 1, 0, HIGH)
        ortho_out[2 * p + 1] = dot(high, high_st, 1, 0, HIGH)
        integrals += [total[p, rank:, :no], total[p, rank:, rank : rank + no]]

    block = cols // n_ta
    for k in range(k_local):
        value = dot(ortho_out[k].astype(BF16), masked[k]).astype(BF16)
        for b in range(n_ta):
            right[b, k] = value[:, b * block : (b + 1) * block]
    fourth = []
    for off in range(1, n_ta):
        to = lax.rem(ta + off, n_ta)
        copy = pltpu.make_async_remote_copy(
            src_ref=right.at[to],
            dst_ref=rights.at[ta],
            send_sem=send4.at[off],
            recv_sem=recv4.at[ta],
            device_id=(ka, to),
            device_id_type=MESH,
        )
        copy.start()
        fourth.append(copy)

    scale = 1.0 / math.sqrt(no * sigma_ref.shape[1] * n_ta)
    for k in range(k_local):
        integral = integrals[k] * scale
        green = dot(gather_a * green_ref[k : k + 1, :], gather_d, 1, 0, HIGH)
        ham = dot(gather_a * ham_ref[k : k + 1, :], gather_d, 1, 0, HIGH)
        for _ in range(2):
            turn = dot(ham, green, 1, 0, HIGH) - dot(green, ham, 1, 0, HIGH)
            green = green + STEP * (turn + integral)
        spread = dot(green, gather_d, 1, 1, HIGH) * gather_a
        green_out[k : k + 1, :] = jnp.sum(spread, axis=0, keepdims=True)

    for copy in third:
        copy.wait_send()
    for off in range(1, n_ta):
        source = lax.rem(ta + off, n_ta)
        pltpu.make_async_remote_copy(
            src_ref=right.at[0],
            dst_ref=rights.at[source],
            send_sem=send4.at[off],
            recv_sem=recv4.at[source],
            device_id=(ka, source),
            device_id_type=MESH,
        ).wait_recv()
    for k in range(k_local):
        value = right[ta, k].astype(F32)
        for off in range(1, n_ta):
            value = value + rights[lax.rem(ta + off, n_ta), k].astype(F32)
        coef_out[k] = value
    for copy in fourth:
        copy.wait_send()


def body(
    n_ka,
    n_ta,
    sigma_history,
    time_basis,
    history_coef,
    green_now,
    hamilton,
    panel_block,
    panel_lengths,
    owners,
    sketch,
):
    k_local, rows, cols = panel_block.shape
    ranks, depth, rank = sketch.shape
    oo = sigma_history.shape[2]
    no = math.isqrt(oo)
    share = ranks // 2 // n_ta
    groups = n_ka // GROUP
    if n_ta == 2:
        whole = cols // no - rows // no // 2
        starts = jnp.where(lax.axis_index("ta") == 0, 0, whole - panel_lengths)
    else:
        every = lax.all_gather(panel_lengths, "ta", tiled=True)
        earlier = jnp.arange(n_ta, dtype=jnp.int32) < lax.axis_index("ta")
        starts = jnp.sum(jnp.where(earlier, every, 0), keepdims=True)
    starts = starts.astype(jnp.int32)
    smem = pl.BlockSpec(memory_space=pltpu.SMEM)
    vmem = pl.BlockSpec(memory_space=pltpu.VMEM)
    hbm = pl.BlockSpec(memory_space=pl.ANY)
    dma = pltpu.SemaphoreType.DMA
    green, ortho, coef = pl.pallas_call(
        functools.partial(kernel, n_ka, n_ta),
        out_shape=(
            jax.ShapeDtypeStruct((k_local, oo), F32),
            jax.ShapeDtypeStruct((k_local, rank, rows), F32),
            jax.ShapeDtypeStruct((k_local, rank, cols // n_ta), F32),
        ),
        in_specs=[smem] * 3 + [vmem] * 2 + [hbm] * 5,
        out_specs=(vmem, vmem, vmem),
        scratch_shapes=[
            pltpu.VMEM(sigma_history.shape, BF16),
            pltpu.VMEM(time_basis.shape[::-1], BF16),
            pltpu.VMEM(history_coef.shape, BF16),
            pltpu.VMEM(panel_block.shape, BF16),
            pltpu.VMEM(sketch.shape, BF16),
            pltpu.VMEM((n_ta, share, depth, 2 * rank), BF16),
            pltpu.VMEM((n_ta, n_ka, share, depth, 2 * rank), BF16),
            pltpu.VMEM(panel_block.shape, BF16),
            pltpu.VMEM((k_local // 2, rank + no, 2 * rank), F32),
            pltpu.VMEM((n_ta, k_local // 2, rank + no, 2 * rank), F32),
            pltpu.VMEM((n_ta, k_local, rank, cols // n_ta), BF16),
            pltpu.VMEM((n_ta, k_local, rank, cols // n_ta), BF16),
            dma((5,)),
            dma((n_ka,)),
            dma((n_ka,)),
            dma((n_ta, groups)),
            dma((n_ta, groups)),
            dma((n_ta,)),
            dma((n_ta,)),
            dma((n_ta,)),
            dma((n_ta,)),
        ],
        compiler_params=pltpu.CompilerParams(
            collective_id=0, has_side_effects=True, vmem_limit_bytes=48 * 1024 * 1024
        ),
    )(
        panel_lengths,
        starts,
        owners.reshape(-1),
        green_now,
        hamilton,
        sigma_history,
        time_basis.T,
        history_coef,
        panel_block,
        sketch,
    )
    return green, ortho.transpose(0, 2, 1), coef


def solution(mesh):
    in_specs = (
        P("ka", "ta", None),
        P("ta", None),
        P("ka", "ta", None),
        P("ka", None),
        P("ka", None),
        P("ka", "ta", None),
        P("ta"),
        P("ka", None),
        P(None, "ka", None),
    )
    out_specs = (P("ka", None), P("ka", "ta", None), P("ka", None, "ta"))
    step = functools.partial(body, mesh.shape["ka"], mesh.shape["ta"])
    return jax.shard_map(step, mesh=mesh, in_specs=in_specs, out_specs=out_specs, check_vma=False)
```

```python
import functools
import math

import jax
import jax.numpy as jnp
from jax import lax
from jax.experimental import pallas as pl
from jax.experimental.pallas import tpu as pltpu
from jax.sharding import PartitionSpec as P

MESH = pl.DeviceIdType.MESH
HIGH = lax.Precision.HIGHEST
F32 = jnp.float32
BF16 = jnp.bfloat16
STEP = 0.25
GROUP = 4


def iota(shape, dim):
    return lax.broadcasted_iota(jnp.int32, shape, dim)


def dot(a, b, da=1, db=0, precision=None):
    return lax.dot_general(
        a, b, (((da,), (db,)), ((), ())), precision=precision, preferred_element_type=F32
    )


def eliminate(mats, offsets, rank):
    count = rank // 8
    full = (8, mats[0].shape[1])
    sub = iota(full, 0)
    tiles = [[m[8 * i : 8 * i + 8] for i in range(count)] for m in mats]
    rows_out = [[] for _ in mats]
    for j in range(count):
        cols = [
            [
                [
                    jnp.broadcast_to(t[i][:, o + 8 * j + a : o + 8 * j + a + 1], full)
                    for a in range(8)
                ]
                for i in range(j, count)
            ]
            for t, o in zip(tiles, offsets)
        ]
        heads = [c[0] for c in cols]
        pivot_rows = [t[j] for t in tiles]
        pivots = [jnp.ones(full, F32) for _ in mats]
        taken = [jnp.zeros(full, F32) for _ in mats]
        for a in range(8):
            for n in range(len(mats)):
                pivot = jnp.broadcast_to(heads[n][a][a : a + 1], full)
                inverse = pl.reciprocal(pivot, approx=False)
                pivots[n] = jnp.where(sub == a, pivot, pivots[n])
                taken[n] = jnp.where(sub == a, pivot_rows[n], taken[n])
                column = heads[n][a]
                for b in range(a + 1, 8):
                    head = heads[n][b]
                    scaled = jnp.broadcast_to(head[a : a + 1], full) * inverse
                    heads[n][b] = jnp.where(sub == a, scaled, head - column * scaled)
                rest = pivot_rows[n]
                scaled = jnp.broadcast_to(rest[a : a + 1], full) * inverse
                pivot_rows[n] = jnp.where(sub == a, scaled, rest - column * scaled)
        for n, t in enumerate(tiles):
            rows_out[n].append(taken[n] * lax.rsqrt(pivots[n]))
            if j + 1 == count:
                continue
            solved = [jnp.broadcast_to(pivot_rows[n][a : a + 1], full) for a in range(8)]
            for i in range(j + 1, count):
                terms = [cols[n][i - j][a] * solved[a] for a in range(8)]
                while len(terms) > 1:
                    terms = [terms[x] + terms[x + 1] for x in range(0, len(terms), 2)]
                t[i] = t[i] - terms[0]
    return [jnp.concatenate(r, axis=0) for r in rows_out]


def kernel(
    n_ka,
    n_ta,
    length_ref,
    owner_hbm,
    green_hbm,
    ham_hbm,
    sigma_hbm,
    basis_hbm,
    hist_hbm,
    panel_hbm,
    sketch_hbm,
    green_out,
    ortho_out,
    coef_out,
    owner_ref,
    green_ref,
    ham_ref,
    sigma_ref,
    basis_ref,
    hist_ref,
    panel_ref,
    sketch_ref,
    packed,
    gathered,
    masked,
    part,
    parts,
    local_sem,
    send1,
    recv1,
    send2,
    recv2,
    send3,
    recv3,
    send4,
    recv4,
):
    ka, ta = lax.axis_index("ka"), lax.axis_index("ta")
    unused, k_local, rows, cols = panel_ref.shape
    ranks, depth, rank = sketch_ref.shape
    share = ranks // 2 // n_ta
    oo = sigma_ref.shape[2]
    no = math.isqrt(oo)
    width = 2 * rank
    block = cols // n_ta

    loads = [
        pltpu.make_async_copy(src, dst, local_sem.at[i])
        for i, (src, dst) in enumerate(
            [
                (sketch_hbm, sketch_ref),
                (basis_hbm, basis_ref),
                (sigma_hbm, sigma_ref),
                (hist_hbm, hist_ref),
                (panel_hbm, panel_ref.at[0]),
                (owner_hbm, owner_ref),
                (green_hbm, green_ref),
                (ham_hbm, ham_ref),
            ]
        )
    ]
    for load in loads:
        load.start()

    barrier = pltpu.get_barrier_semaphore()
    for off in range(1, n_ka):
        pl.semaphore_signal(
            barrier, inc=1, device_id=(lax.rem(ka + off, n_ka), ta), device_id_type=MESH
        )
    for off in range(1, n_ta):
        pl.semaphore_signal(
            barrier, inc=1, device_id=(ka, lax.rem(ta + off, n_ta)), device_id_type=MESH
        )
    loads[0].wait()
    for pair in range(ranks // 2):
        packed[pair // share, pair % share] = jnp.concatenate(
            [sketch_ref[2 * pair], sketch_ref[2 * pair + 1]], axis=1
        )
    gathered[ta, ka] = packed[ta]
    pl.semaphore_wait(barrier, n_ka - 1 + n_ta - 1)

    first = []
    for off in range(n_ka - 1, 0, -1):
        to = lax.rem(ka + off, n_ka)
        copy = pltpu.make_async_remote_copy(
            src_ref=packed.at[ta],
            dst_ref=gathered.at[ta, ka],
            send_sem=send1.at[off],
            recv_sem=recv1.at[ka],
            device_id=(to, ta),
            device_id_type=MESH,
        )
        copy.start()
        first.append(copy)

    panels = []
    for off in range(1, n_ta):
        copy = pltpu.make_async_remote_copy(
            src_ref=panel_hbm,
            dst_ref=panel_ref.at[n_ta - off],
            send_sem=send4.at[off],
            recv_sem=recv4.at[n_ta - off],
            device_id=(ka, lax.rem(ta + off, n_ta)),
            device_id_type=MESH,
        )
        copy.start()
        panels.append(copy)

    gather_a = jnp.where(lax.div(iota((no, oo), 1), no) == iota((no, oo), 0), 1.0, 0.0)
    gather_d = jnp.where(lax.rem(iota((oo, no), 0), no) == iota((oo, no), 1), 1.0, 0.0)
    diag = lax.rem(iota((oo, oo), 0), no) == lax.div(iota((oo, oo), 1), no)
    for load in loads[1:4]:
        load.wait()
    basis = basis_ref[...]
    for k in range(k_local):
        summed = dot(basis, sigma_ref[k])
        outer = dot(summed, hist_ref[k].astype(F32), 0, 0, HIGH)
        outer = jnp.where(diag, outer, 0.0)
        part[k] = dot(dot(gather_a, outer, 1, 0, HIGH), gather_d, 1, 0, HIGH)
    third = []
    for off in range(1, n_ta):
        copy = pltpu.make_async_remote_copy(
            src_ref=part,
            dst_ref=parts.at[n_ta - off],
            send_sem=send3.at[off],
            recv_sem=recv3.at[n_ta - off],
            device_id=(ka, lax.rem(ta + off, n_ta)),
            device_id_type=MESH,
        )
        copy.start()
        third.append(copy)

    slots = rows // no
    if n_ta == 2:
        mine = length_ref[0]
        whole = cols // no - slots // 2
        lengths = [mine, whole - mine]
        starts = [jnp.where(ta == 0, 0, whole - mine), jnp.where(ta == 0, mine, 0)]
    else:
        lengths, starts = [], []
        for off in range(n_ta):
            at = lax.rem(ta + off, n_ta)
            length, start = jnp.int32(0), jnp.int32(0)
            for b in range(n_ta):
                length = jnp.where(at == b, length_ref[b], length)
                start = start + jnp.where(b < at, length_ref[b], 0)
            lengths.append(length)
            starts.append(start)
    row = iota((rows, cols), 0)
    lead = iota((rows, cols), 1) - lax.div(row, no) * no

    def mask(off):
        keep = (lead < (starts[off] + slots // 2 + 1) * no) & (row < lengths[off] * no)
        unit = jnp.where(keep, 1.0, 0.0).astype(BF16)
        for k in range(k_local):
            masked[off, k] = panel_ref[off, k] * unit

    loads[4].wait()
    mask(0)

    groups = n_ka // GROUP
    second = []
    home = lax.div(ka, GROUP)
    for g in range(groups):
        group = lax.rem(home + g, groups)
        for i in range(GROUP):
            source = group * GROUP + i

            @pl.when(source != ka)
            def _():
                pltpu.make_async_remote_copy(
                    src_ref=packed.at[ta],
                    dst_ref=gathered.at[ta, source],
                    send_sem=send1.at[0],
                    recv_sem=recv1.at[source],
                    device_id=(ka, lax.rem(ta + 1, n_ta)),
                    device_id_type=MESH,
                ).wait_recv()

        for off in range(1, n_ta):
            piece = gathered.at[ta, pl.ds(group * GROUP, GROUP)]
            copy = pltpu.make_async_remote_copy(
                src_ref=piece,
                dst_ref=piece,
                send_sem=send2.at[off, g],
                recv_sem=recv2.at[ta, group],
                device_id=(ka, lax.rem(ta + off, n_ta)),
                device_id_type=MESH,
            )
            copy.start()
            second.append(copy)

    for load in loads[5:]:
        load.wait()
    for off in range(1, n_ta):
        pltpu.make_async_remote_copy(
            src_ref=panel_hbm,
            dst_ref=panel_ref.at[off],
            send_sem=send4.at[off],
            recv_sem=recv4.at[off],
            device_id=(ka, lax.rem(ta + off, n_ta)),
            device_id_type=MESH,
        ).wait_recv()
        mask(off)
        pltpu.make_async_remote_copy(
            src_ref=part,
            dst_ref=parts.at[off],
            send_sem=send3.at[off],
            recv_sem=recv3.at[off],
            device_id=(ka, lax.rem(ta + off, n_ta)),
            device_id_type=MESH,
        ).wait_recv()

    for off in range(1, n_ta):
        source = lax.rem(ta + off, n_ta)
        for g in range(groups):
            piece = gathered.at[source, pl.ds(g * GROUP, GROUP)]
            pltpu.make_async_remote_copy(
                src_ref=piece,
                dst_ref=piece,
                send_sem=send2.at[off, g],
                recv_sem=recv2.at[source, g],
                device_id=(ka, source),
                device_id_type=MESH,
            ).wait_recv()

    sketched = []
    grams = []
    for k in range(k_local):
        owner = owner_ref[k]
        pair = lax.div(owner, 2)
        omega = gathered[lax.div(pair, share), :, lax.rem(pair, share)]
        omega = omega.reshape(n_ka * depth, width)
        values = []
        for off in range(n_ta):
            both = dot(omega, masked[off, k], 0, 1)
            values.append(jnp.where(lax.rem(owner, 2) == 0, both[:rank], both[rank:]))
        sketched.append(values)
        gram = dot(values[0], values[0], 1, 1, HIGH)
        for value in values[1:]:
            gram = gram + dot(value, value, 1, 1, HIGH)
        grams.append(gram)

    lane = iota((rank, width), 1)
    line = iota((rank, width), 0)
    inverses = []
    for p in range(k_local // 2):
        gram = jnp.concatenate([grams[2 * p], grams[2 * p + 1]], axis=1)
        left = jnp.where(lane < rank, gram, jnp.where(lane == line + rank, 1.0, 0.0))
        other = jnp.where(lane >= rank, gram, jnp.where(lane == line, 1.0, 0.0))
        low, high = eliminate([left, other], [0, rank], rank)
        inverses += [jnp.where(lane >= rank, low, 0.0), jnp.where(lane < rank, high, 0.0)]

    empty = jnp.zeros((rank, rows), F32)
    mine = pl.ds(pl.multiple_of(ta * block, block), block)
    for k in range(k_local):
        total = jnp.zeros((rank, block), F32)
        for off in range(n_ta):
            value = sketched[k][off]
            stack = [empty, value] if k % 2 == 0 else [value, empty]
            ortho = dot(inverses[k], jnp.concatenate(stack, axis=0), 1, 0, HIGH)
            if off == 0:
                ortho_out[k] = ortho
            piece = dot(ortho.astype(BF16), masked[off, k, :, mine])
            total = total + piece.astype(BF16).astype(F32)
        coef_out[k] = total

    scale = 1.0 / math.sqrt(no * sigma_ref.shape[1] * n_ta)
    for k in range(k_local):
        integral = part[k]
        for off in range(1, n_ta):
            integral = integral + parts[off, k]
        integral = integral * scale
        green = dot(gather_a * green_ref[k : k + 1, :], gather_d, 1, 0, HIGH)
        ham = dot(gather_a * ham_ref[k : k + 1, :], gather_d, 1, 0, HIGH)
        for _ in range(2):
            turn = dot(ham, green, 1, 0, HIGH) - dot(green, ham, 1, 0, HIGH)
            green = green + STEP * (turn + integral)
        spread = dot(green, gather_d, 1, 1, HIGH) * gather_a
        green_out[k : k + 1, :] = jnp.sum(spread, axis=0, keepdims=True)

    for copy in first + second + third + panels:
        copy.wait_send()


def finish(green_ref, ortho_ref, coef_ref, green_hbm, ortho_hbm, coef_hbm, sem):
    moves = [
        pltpu.make_async_copy(coef_ref, coef_hbm, sem.at[0]),
        pltpu.make_async_copy(ortho_ref, ortho_hbm, sem.at[1]),
        pltpu.make_async_copy(green_ref, green_hbm, sem.at[2]),
    ]
    for move in moves:
        move.start()
    for move in moves:
        move.wait()


def body(
    n_ka,
    n_ta,
    sigma_history,
    time_basis,
    history_coef,
    green_now,
    hamilton,
    panel_block,
    panel_lengths,
    owners,
    sketch,
):
    k_local, rows, cols = panel_block.shape
    ranks, depth, rank = sketch.shape
    oo = sigma_history.shape[2]
    no = math.isqrt(oo)
    share = ranks // 2 // n_ta
    groups = n_ka // GROUP
    lengths = panel_lengths
    if n_ta > 2:
        lengths = lax.all_gather(panel_lengths, "ta", tiled=True)
    smem = pl.BlockSpec(memory_space=pltpu.SMEM)
    vmem = pl.BlockSpec(memory_space=pltpu.VMEM)
    hbm = pl.BlockSpec(memory_space=pltpu.HBM)
    dma = pltpu.SemaphoreType.DMA
    outs = (
        jax.ShapeDtypeStruct((k_local, oo), F32),
        jax.ShapeDtypeStruct((k_local, rank, rows), F32),
        jax.ShapeDtypeStruct((k_local, rank, cols // n_ta), F32),
    )
    results = pl.pallas_call(
        functools.partial(kernel, n_ka, n_ta),
        out_shape=outs,
        in_specs=[smem] + [hbm] * 8,
        out_specs=(vmem, vmem, vmem),
        scratch_shapes=[
            pltpu.SMEM((k_local,), jnp.int32),
            pltpu.VMEM(green_now.shape, F32),
            pltpu.VMEM(green_now.shape, F32),
            pltpu.VMEM(sigma_history.shape, BF16),
            pltpu.VMEM(time_basis.shape[::-1], BF16),
            pltpu.VMEM(history_coef.shape, BF16),
            pltpu.VMEM((n_ta,) + panel_block.shape, BF16),
            pltpu.VMEM(sketch.shape, BF16),
            pltpu.VMEM((n_ta, share, depth, 2 * rank), BF16),
            pltpu.VMEM((n_ta, n_ka, share, depth, 2 * rank), BF16),
            pltpu.VMEM((n_ta,) + panel_block.shape, BF16),
            pltpu.VMEM((k_local, no, no), F32),
            pltpu.VMEM((n_ta, k_local, no, no), F32),
            dma((8,)),
            dma((n_ka,)),
            dma((n_ka,)),
            dma((n_ta, groups)),
            dma((n_ta, groups)),
            dma((n_ta,)),
            dma((n_ta,)),
            dma((n_ta,)),
            dma((n_ta,)),
        ],
        compiler_params=pltpu.CompilerParams(
            collective_id=0, has_side_effects=True, vmem_limit_bytes=56 * 1024 * 1024
        ),
    )(
        lengths,
        *[
            pltpu.with_memory_space_constraint(x, pltpu.HBM)
            for x in (
                owners.reshape(-1),
                green_now,
                hamilton,
                sigma_history,
                time_basis.T,
                history_coef,
                panel_block,
                sketch,
            )
        ],
    )
    green, ortho, coef = pl.pallas_call(
        finish,
        out_shape=outs,
        in_specs=[vmem] * 3,
        out_specs=(hbm, hbm, hbm),
        scratch_shapes=[dma((3,))],
        compiler_params=pltpu.CompilerParams(vmem_limit_bytes=8 * 1024 * 1024),
    )(*results)
    return green, ortho.transpose(0, 2, 1), coef


def solution(mesh):
    in_specs = (
        P("ka", "ta", None),
        P("ta", None),
        P("ka", "ta", None),
        P("ka", None),
        P("ka", None),
        P("ka", "ta", None),
        P("ta"),
        P("ka", None),
        P(None, "ka", None),
    )
    out_specs = (P("ka", None), P("ka", "ta", None), P("ka", None, "ta"))
    step = functools.partial(body, mesh.shape["ka"], mesh.shape["ta"])
    return jax.shard_map(step, mesh=mesh, in_specs=in_specs, out_specs=out_specs, check_vma=False)
```

```python
import functools
import math

import jax
import jax.numpy as jnp
from jax import lax
from jax.experimental import pallas as pl
from jax.experimental.pallas import tpu as pltpu
from jax.sharding import PartitionSpec as P

MESH = pl.DeviceIdType.MESH
HIGH = lax.Precision.HIGHEST
F32 = jnp.float32
BF16 = jnp.bfloat16
STEP = 0.25
GROUP = 4


def iota(shape, dim):
    return lax.broadcasted_iota(jnp.int32, shape, dim)


def dot(a, b, da=1, db=0, precision=None):
    return lax.dot_general(
        a, b, (((da,), (db,)), ((), ())), precision=precision, preferred_element_type=F32
    )


def halves(x):
    high = x.astype(BF16)
    return high, (x - high.astype(F32)).astype(BF16)


def fold(x, no):
    y = x[:, :128]
    for i in range(1, x.shape[1] // 128):
        y = y + x[:, 128 * i : 128 * (i + 1)]
    shift = 64
    while shift >= no:
        y = y + pltpu.roll(y, shift, 1)
        shift //= 2
    return y


def eliminate(mats, offsets, rank):
    count = rank // 8
    full = (8, mats[0].shape[1])
    sub = iota(full, 0)
    tiles = [[m[8 * i : 8 * i + 8] for i in range(count)] for m in mats]
    rows_out = [[] for _ in mats]
    for j in range(count):
        cols = [
            [
                [
                    jnp.broadcast_to(t[i][:, o + 8 * j + a : o + 8 * j + a + 1], full)
                    for a in range(8)
                ]
                for i in range(j, count)
            ]
            for t, o in zip(tiles, offsets)
        ]
        heads = [c[0] for c in cols]
        pivot_rows = [t[j] for t in tiles]
        pivots = [jnp.ones(full, F32) for _ in mats]
        taken = [jnp.zeros(full, F32) for _ in mats]
        for a in range(8):
            for n in range(len(mats)):
                pivot = jnp.broadcast_to(heads[n][a][a : a + 1], full)
                inverse = pl.reciprocal(pivot, approx=False)
                pivots[n] = jnp.where(sub == a, pivot, pivots[n])
                taken[n] = jnp.where(sub == a, pivot_rows[n], taken[n])
                column = heads[n][a]
                for b in range(a + 1, 8):
                    head = heads[n][b]
                    scaled = jnp.broadcast_to(head[a : a + 1], full) * inverse
                    heads[n][b] = jnp.where(sub == a, scaled, head - column * scaled)
                rest = pivot_rows[n]
                scaled = jnp.broadcast_to(rest[a : a + 1], full) * inverse
                pivot_rows[n] = jnp.where(sub == a, scaled, rest - column * scaled)
        for n, t in enumerate(tiles):
            rows_out[n].append(taken[n] * lax.rsqrt(pivots[n]))
            if j + 1 == count:
                continue
            solved = [jnp.broadcast_to(pivot_rows[n][a : a + 1], full) for a in range(8)]
            for i in range(j + 1, count):
                terms = [cols[n][i - j][a] * solved[a] for a in range(8)]
                while len(terms) > 1:
                    terms = [terms[x] + terms[x + 1] for x in range(0, len(terms), 2)]
                t[i] = t[i] - terms[0]
    return [jnp.concatenate(r, axis=0) for r in rows_out]


def kernel(
    n_ka,
    n_ta,
    length_ref,
    owner_hbm,
    green_hbm,
    ham_hbm,
    sigma_hbm,
    basis_hbm,
    hist_hbm,
    panel_hbm,
    sketch_hbm,
    green_hbm_out,
    ortho_hbm_out,
    coef_hbm_out,
    green_out,
    ortho_out,
    coef_out,
    owner_ref,
    green_ref,
    ham_ref,
    sigma_ref,
    basis_ref,
    hist_ref,
    panel_ref,
    sketch_ref,
    packed,
    gathered,
    masked,
    part,
    parts,
    local_sem,
    out_sem,
    send1,
    recv1,
    send2,
    recv2,
    send3,
    recv3,
    send4,
    recv4,
):
    ka, ta = lax.axis_index("ka"), lax.axis_index("ta")
    unused, k_local, rows, cols = panel_ref.shape
    ranks, depth, rank = sketch_ref.shape
    share = ranks // 2 // n_ta
    oo = sigma_ref.shape[2]
    no = math.isqrt(oo)
    width = 2 * rank
    block = cols // n_ta

    loads = [
        pltpu.make_async_copy(src, dst, local_sem.at[i])
        for i, (src, dst) in enumerate(
            [
                (sketch_hbm, sketch_ref),
                (basis_hbm, basis_ref),
                (sigma_hbm, sigma_ref),
                (hist_hbm, hist_ref),
                (panel_hbm, panel_ref.at[0]),
                (owner_hbm, owner_ref),
                (green_hbm, green_ref),
                (ham_hbm, ham_ref),
            ]
        )
    ]
    for load in loads:
        load.start()

    barrier = pltpu.get_barrier_semaphore()
    for off in range(1, n_ka):
        pl.semaphore_signal(
            barrier, inc=1, device_id=(lax.rem(ka + off, n_ka), ta), device_id_type=MESH
        )
    for off in range(1, n_ta):
        pl.semaphore_signal(
            barrier, inc=1, device_id=(ka, lax.rem(ta + off, n_ta)), device_id_type=MESH
        )
    loads[0].wait()
    for pair in range(ranks // 2):
        packed[pair // share, pair % share] = jnp.concatenate(
            [sketch_ref[2 * pair], sketch_ref[2 * pair + 1]], axis=1
        )
    gathered[ta, ka] = packed[ta]
    pl.semaphore_wait(barrier, n_ka - 1 + n_ta - 1)

    first = []
    for off in range(n_ka - 1, 0, -1):
        to = lax.rem(ka + off, n_ka)
        copy = pltpu.make_async_remote_copy(
            src_ref=packed.at[ta],
            dst_ref=gathered.at[ta, ka],
            send_sem=send1.at[off],
            recv_sem=recv1.at[ka],
            device_id=(to, ta),
            device_id_type=MESH,
        )
        copy.start()
        first.append(copy)

    panels, moves = [], []
    for off in range(1, n_ta):
        copy = pltpu.make_async_remote_copy(
            src_ref=panel_hbm,
            dst_ref=panel_ref.at[n_ta - off],
            send_sem=send4.at[off],
            recv_sem=recv4.at[n_ta - off],
            device_id=(ka, lax.rem(ta + off, n_ta)),
            device_id_type=MESH,
        )
        copy.start()
        panels.append(copy)

    own = lax.div(iota((no, oo), 1), no) == iota((no, oo), 0)
    diag = lax.rem(iota((oo, oo), 0), no) == lax.div(iota((oo, oo), 1), no)
    for load in loads[1:4]:
        load.wait()
    basis = basis_ref[...]
    for k in range(k_local):
        summed = jnp.concatenate(halves(dot(basis, sigma_ref[k])), axis=0)
        coef = jnp.concatenate([hist_ref[k], hist_ref[k]], axis=0)
        outer = jnp.where(diag, dot(summed, coef, 0, 0), 0.0)
        part[k] = fold(jnp.sum(outer.reshape(no, no, oo), axis=1), no)
    third = []
    for off in range(1, n_ta):
        copy = pltpu.make_async_remote_copy(
            src_ref=part,
            dst_ref=parts.at[n_ta - off],
            send_sem=send3.at[off],
            recv_sem=recv3.at[n_ta - off],
            device_id=(ka, lax.rem(ta + off, n_ta)),
            device_id_type=MESH,
        )
        copy.start()
        third.append(copy)

    slots = rows // no
    if n_ta == 2:
        mine = length_ref[0]
        whole = cols // no - slots // 2
        lengths = [mine, whole - mine]
        starts = [jnp.where(ta == 0, 0, whole - mine), jnp.where(ta == 0, mine, 0)]
    else:
        lengths, starts = [], []
        for off in range(n_ta):
            at = lax.rem(ta + off, n_ta)
            length, start = jnp.int32(0), jnp.int32(0)
            for b in range(n_ta):
                length = jnp.where(at == b, length_ref[b], length)
                start = start + jnp.where(b < at, length_ref[b], 0)
            lengths.append(length)
            starts.append(start)
    row = iota((rows, cols), 0)
    lead = iota((rows, cols), 1) - lax.div(row, no) * no

    def mask(off):
        keep = (lead < (starts[off] + slots // 2 + 1) * no) & (row < lengths[off] * no)
        unit = jnp.where(keep, 1.0, 0.0).astype(BF16)
        for k in range(k_local):
            masked[off, k] = panel_ref[off, k] * unit

    loads[4].wait()
    mask(0)

    groups = n_ka // GROUP
    second = []
    home = lax.div(ka, GROUP)
    for g in range(groups):
        group = lax.rem(home + g, groups)
        for i in range(GROUP):
            source = group * GROUP + i

            @pl.when(source != ka)
            def _():
                pltpu.make_async_remote_copy(
                    src_ref=packed.at[ta],
                    dst_ref=gathered.at[ta, source],
                    send_sem=send1.at[0],
                    recv_sem=recv1.at[source],
                    device_id=(ka, lax.rem(ta + 1, n_ta)),
                    device_id_type=MESH,
                ).wait_recv()

        for off in range(1, n_ta):
            piece = gathered.at[ta, pl.ds(group * GROUP, GROUP)]
            copy = pltpu.make_async_remote_copy(
                src_ref=piece,
                dst_ref=piece,
                send_sem=send2.at[off, g],
                recv_sem=recv2.at[ta, group],
                device_id=(ka, lax.rem(ta + off, n_ta)),
                device_id_type=MESH,
            )
            copy.start()
            second.append(copy)

    for load in loads[5:]:
        load.wait()
    for off in range(1, n_ta):
        pltpu.make_async_remote_copy(
            src_ref=panel_hbm,
            dst_ref=panel_ref.at[off],
            send_sem=send4.at[off],
            recv_sem=recv4.at[off],
            device_id=(ka, lax.rem(ta + off, n_ta)),
            device_id_type=MESH,
        ).wait_recv()
        mask(off)
        pltpu.make_async_remote_copy(
            src_ref=part,
            dst_ref=parts.at[off],
            send_sem=send3.at[off],
            recv_sem=recv3.at[off],
            device_id=(ka, lax.rem(ta + off, n_ta)),
            device_id_type=MESH,
        ).wait_recv()

    scale = 1.0 / math.sqrt(no * sigma_ref.shape[1] * n_ta)
    for k in range(k_local):
        integral = part[k]
        for off in range(1, n_ta):
            integral = integral + parts[off, k]
        integral = integral * scale
        green = fold(jnp.where(own, green_ref[k : k + 1, :], 0.0), no)
        ham = fold(jnp.where(own, ham_ref[k : k + 1, :], 0.0), no)
        for _ in range(2):
            turn = dot(ham[:, :no], green, 1, 0, HIGH) - dot(green[:, :no], ham, 1, 0, HIGH)
            green = green + STEP * (turn + integral)
        spread = jnp.where(own, jnp.concatenate([green] * (oo // 128), axis=1), 0.0)
        green_out[k : k + 1, :] = jnp.sum(spread, axis=0, keepdims=True)
    moves.append(pltpu.make_async_copy(green_out, green_hbm_out, out_sem.at[2 * k_local]))
    moves[-1].start()

    for off in range(1, n_ta):
        source = lax.rem(ta + off, n_ta)
        for g in range(groups):
            piece = gathered.at[source, pl.ds(g * GROUP, GROUP)]
            pltpu.make_async_remote_copy(
                src_ref=piece,
                dst_ref=piece,
                send_sem=send2.at[off, g],
                recv_sem=recv2.at[source, g],
                device_id=(ka, source),
                device_id_type=MESH,
            ).wait_recv()

    sketched = []
    grams = []
    for k in range(k_local):
        owner = owner_ref[k]
        pair = lax.div(owner, 2)
        omega = gathered[lax.div(pair, share), :, lax.rem(pair, share)]
        omega = omega.reshape(n_ka * depth, width)
        values = []
        for off in range(n_ta):
            both = dot(omega, masked[off, k], 0, 1)
            values.append(jnp.where(lax.rem(owner, 2) == 0, both[:rank], both[rank:]))
        sketched.append(values)
        gram = jnp.zeros((width, width), F32)
        for off in range(n_ta):
            values[off] = jnp.concatenate(halves(values[off]), axis=0)
            gram = gram + dot(values[off], values[off], 1, 1)
        gram = gram[:rank] + gram[rank:]
        grams.append(gram + pltpu.roll(gram, rank, 1))

    lane = iota((rank, width), 1)
    line = iota((rank, width), 0)
    mats = [jnp.where(lane < rank, g, jnp.where(lane == line + rank, 1.0, 0.0)) for g in grams]
    inverses = []
    for inverse in eliminate(mats, [0] * k_local, rank):
        inverse = jnp.where(lane >= rank, inverse, 0.0)
        inverse = inverse + pltpu.roll(inverse, rank, 1)
        inverses.append(jnp.concatenate(halves(inverse), axis=0))

    mine = pl.ds(pl.multiple_of(ta * block, block), block)
    for k in range(k_local):
        total = jnp.zeros((rank, block), F32)
        for off in range(n_ta):
            ortho = dot(inverses[k], sketched[k][off])
            ortho = ortho[:rank] + ortho[rank:]
            if off == 0:
                ortho_out[k] = ortho
                move = pltpu.make_async_copy(ortho_out.at[k], ortho_hbm_out.at[k], out_sem.at[k])
                move.start()
                moves.append(move)
            piece = dot(ortho.astype(BF16), masked[off, k, :, mine])
            total = total + piece.astype(BF16).astype(F32)
        coef_out[k] = total
        place = k_local + k
        move = pltpu.make_async_copy(coef_out.at[k], coef_hbm_out.at[k], out_sem.at[place])
        move.start()
        moves.append(move)

    for copy in first + second + third + panels:
        copy.wait_send()
    for move in moves:
        move.wait()


def finish(green_ref, ortho_ref, coef_ref, green_hbm, ortho_hbm, coef_hbm, sem):
    moves = [
        pltpu.make_async_copy(coef_ref, coef_hbm, sem.at[0]),
        pltpu.make_async_copy(ortho_ref, ortho_hbm, sem.at[1]),
        pltpu.make_async_copy(green_ref, green_hbm, sem.at[2]),
    ]
    for move in moves:
        move.start()
    for move in moves:
        move.wait()


def body(
    n_ka,
    n_ta,
    sigma_history,
    time_basis,
    history_coef,
    green_now,
    hamilton,
    panel_block,
    panel_lengths,
    owners,
    sketch,
):
    k_local, rows, cols = panel_block.shape
    ranks, depth, rank = sketch.shape
    oo = sigma_history.shape[2]
    no = math.isqrt(oo)
    share = ranks // 2 // n_ta
    groups = n_ka // GROUP
    lengths = panel_lengths
    if n_ta > 2:
        lengths = lax.all_gather(panel_lengths, "ta", tiled=True)
    smem = pl.BlockSpec(memory_space=pltpu.SMEM)
    hbm = pl.BlockSpec(memory_space=pltpu.HBM)
    dma = pltpu.SemaphoreType.DMA
    outs = (
        jax.ShapeDtypeStruct((k_local, oo), F32),
        jax.ShapeDtypeStruct((k_local, rank, rows), F32),
        jax.ShapeDtypeStruct((k_local, rank, cols // n_ta), F32),
    )
    results = pl.pallas_call(
        functools.partial(kernel, n_ka, n_ta),
        out_shape=outs,
        in_specs=[smem] + [hbm] * 8,
        out_specs=(hbm, hbm, hbm),
        scratch_shapes=[
            *[pltpu.VMEM(x.shape, F32) for x in outs],
            pltpu.SMEM((k_local,), jnp.int32),
            pltpu.VMEM(green_now.shape, F32),
            pltpu.VMEM(green_now.shape, F32),
            pltpu.VMEM(sigma_history.shape, BF16),
            pltpu.VMEM(time_basis.shape[::-1], BF16),
            pltpu.VMEM(history_coef.shape, BF16),
            pltpu.VMEM((n_ta,) + panel_block.shape, BF16),
            pltpu.VMEM(sketch.shape, BF16),
            pltpu.VMEM((n_ta, share, depth, 2 * rank), BF16),
            pltpu.VMEM((n_ta, n_ka, share, depth, 2 * rank), BF16),
            pltpu.VMEM((n_ta,) + panel_block.shape, BF16),
            pltpu.VMEM((k_local, no, 128), F32),
            pltpu.VMEM((n_ta, k_local, no, 128), F32),
            dma((8,)),
            dma((2 * k_local + 1,)),
            dma((n_ka,)),
            dma((n_ka,)),
            dma((n_ta, groups)),
            dma((n_ta, groups)),
            dma((n_ta,)),
            dma((n_ta,)),
            dma((n_ta,)),
            dma((n_ta,)),
        ],
        compiler_params=pltpu.CompilerParams(
            collective_id=0, has_side_effects=True, vmem_limit_bytes=56 * 1024 * 1024
        ),
    )(
        lengths,
        *[
            pltpu.with_memory_space_constraint(x, pltpu.HBM)
            for x in (
                owners.reshape(-1),
                green_now,
                hamilton,
                sigma_history,
                time_basis.T,
                history_coef,
                panel_block,
                sketch,
            )
        ],
    )
    green, ortho, coef = pl.pallas_call(
        finish,
        out_shape=outs,
        in_specs=[hbm] * 3,
        out_specs=(hbm, hbm, hbm),
        scratch_shapes=[dma((3,))],
        compiler_params=pltpu.CompilerParams(vmem_limit_bytes=8 * 1024 * 1024),
    )(*[pltpu.with_memory_space_constraint(x, pltpu.HBM) for x in results])
    return green, ortho.transpose(0, 2, 1), coef


def solution(mesh):
    in_specs = (
        P("ka", "ta", None),
        P("ta", None),
        P("ka", "ta", None),
        P("ka", None),
        P("ka", None),
        P("ka", "ta", None),
        P("ta"),
        P("ka", None),
        P(None, "ka", None),
    )
    out_specs = (P("ka", None), P("ka", "ta", None), P("ka", None, "ta"))
    step = functools.partial(body, mesh.shape["ka"], mesh.shape["ta"])
    return jax.shard_map(step, mesh=mesh, in_specs=in_specs, out_specs=out_specs, check_vma=False)
```

```python
import functools
import math

import jax
import jax.numpy as jnp
from jax import lax
from jax.experimental import pallas as pl
from jax.experimental.pallas import tpu as pltpu
from jax.sharding import PartitionSpec as P

MESH = pl.DeviceIdType.MESH
HIGH = lax.Precision.HIGHEST
F32 = jnp.float32
BF16 = jnp.bfloat16
STEP = 0.25


def iota(shape, dim):
    return lax.broadcasted_iota(jnp.int32, shape, dim)


def dot(a, b, da=1, db=0, precision=None):
    return lax.dot_general(
        a, b, (((da,), (db,)), ((), ())), precision=precision, preferred_element_type=F32
    )


def halves(x):
    high = x.astype(BF16)
    return high, (x - high.astype(F32)).astype(BF16)


def fold(x, no):
    y = x[:, :128]
    for i in range(1, x.shape[1] // 128):
        y = y + x[:, 128 * i : 128 * (i + 1)]
    shift = 64
    while shift >= no:
        y = y + pltpu.roll(y, shift, 1)
        shift //= 2
    return y


def eliminate(mats, offsets, rank):
    count = rank // 8
    full = (8, mats[0].shape[1])
    sub = iota(full, 0)
    tiles = [[m[8 * i : 8 * i + 8] for i in range(count)] for m in mats]
    rows_out = [[] for _ in mats]
    for j in range(count):
        cols = [
            [
                [
                    jnp.broadcast_to(t[i][:, o + 8 * j + a : o + 8 * j + a + 1], full)
                    for a in range(8)
                ]
                for i in range(j, count)
            ]
            for t, o in zip(tiles, offsets)
        ]
        count_of = range(len(mats))
        block = [
            [[jnp.broadcast_to(c[0][b][a : a + 1], full) for b in range(8)] for a in range(8)]
            for c in cols
        ]
        rows = [[jnp.broadcast_to(t[j][a : a + 1], full) for a in range(8)] for t in tiles]
        inverse = [[None] * 8 for _ in mats]
        for a in range(8):
            for n in count_of:
                v, r = block[n], rows[n]
                inverse[n][a] = pl.reciprocal(v[a][a], approx=False)
                for b in range(a + 1, 8):
                    factor = v[a][b] * inverse[n][a]
                    v[b][a] = factor
                    for c in range(b, 8):
                        v[b][c] = v[b][c] - factor * v[a][c]
                    r[b] = r[b] - factor * r[a]
        for n, t in enumerate(tiles):
            v, r = block[n], rows[n]
            pivot, taken = v[7][7], r[7]
            for a in range(7):
                pivot = jnp.where(sub == a, v[a][a], pivot)
                taken = jnp.where(sub == a, r[a], taken)
            rows_out[n].append(taken * lax.rsqrt(pivot))
            if j + 1 == count:
                continue
            solved = [x * i for x, i in zip(r, inverse[n])]
            for b in range(7, 0, -1):
                for a in range(b):
                    solved[a] = solved[a] - v[b][a] * solved[b]
            for i in range(j + 1, count):
                terms = [cols[n][i - j][a] * solved[a] for a in range(8)]
                while len(terms) > 1:
                    terms = [terms[x] + terms[x + 1] for x in range(0, len(terms), 2)]
                t[i] = t[i] - terms[0]
    return [jnp.concatenate(r, axis=0) for r in rows_out]


def kernel(
    n_ka,
    n_ta,
    length_ref,
    owner_hbm,
    green_hbm,
    ham_hbm,
    sigma_hbm,
    basis_hbm,
    hist_hbm,
    panel_hbm,
    sketch_hbm,
    green_hbm_out,
    ortho_hbm_out,
    coef_hbm_out,
    green_out,
    ortho_out,
    coef_out,
    owner_ref,
    green_ref,
    ham_ref,
    sigma_ref,
    basis_ref,
    hist_ref,
    panel_ref,
    sketch_ref,
    packed,
    gathered,
    masked,
    part,
    parts,
    local_sem,
    out_sem,
    send1,
    recv1,
    send2,
    recv2,
    send3,
    recv3,
    send4,
    recv4,
):
    ka, ta = lax.axis_index("ka"), lax.axis_index("ta")
    unused, k_local, rows, cols = panel_ref.shape
    ranks, depth, rank = sketch_ref.shape
    share = ranks // 2 // n_ta
    oo = sigma_ref.shape[2]
    no = math.isqrt(oo)
    width = 2 * rank
    block = cols // n_ta

    loads = [
        pltpu.make_async_copy(src, dst, local_sem.at[i])
        for i, (src, dst) in enumerate(
            [
                (sketch_hbm, sketch_ref),
                (basis_hbm, basis_ref),
                (sigma_hbm, sigma_ref),
                (hist_hbm, hist_ref),
                (panel_hbm, panel_ref.at[0]),
                (owner_hbm, owner_ref),
                (green_hbm, green_ref),
                (ham_hbm, ham_ref),
            ]
        )
    ]
    loads[0].start()

    barrier = pltpu.get_barrier_semaphore()
    for off in range(1, n_ka):
        pl.semaphore_signal(
            barrier, inc=1, device_id=(lax.rem(ka + off, n_ka), ta), device_id_type=MESH
        )
    for off in range(1, n_ta):
        pl.semaphore_signal(
            barrier, inc=1, device_id=(ka, lax.rem(ta + off, n_ta)), device_id_type=MESH
        )
    for load in loads[1:]:
        load.start()
    loads[0].wait()
    for pair in range(ranks // 2):
        packed[pair // share, pair % share] = jnp.concatenate(
            [sketch_ref[2 * pair], sketch_ref[2 * pair + 1]], axis=1
        )
    gathered[ta, ka] = packed[ta]
    pl.semaphore_wait(barrier, n_ka - 1 + n_ta - 1)

    first = []
    for off in range(n_ka - 1, 0, -1):
        to = lax.rem(ka + off, n_ka)
        copy = pltpu.make_async_remote_copy(
            src_ref=packed.at[ta],
            dst_ref=gathered.at[ta, ka],
            send_sem=send1.at[off],
            recv_sem=recv1.at[ka],
            device_id=(to, ta),
            device_id_type=MESH,
        )
        copy.start()
        first.append(copy)

    panels, moves = [], []
    for off in range(1, n_ta):
        copy = pltpu.make_async_remote_copy(
            src_ref=panel_hbm,
            dst_ref=panel_ref.at[n_ta - off],
            send_sem=send4.at[off],
            recv_sem=recv4.at[n_ta - off],
            device_id=(ka, lax.rem(ta + off, n_ta)),
            device_id_type=MESH,
        )
        copy.start()
        panels.append(copy)

    own = lax.div(iota((no, oo), 1), no) == iota((no, oo), 0)
    diag = lax.rem(iota((oo, oo), 0), no) == lax.div(iota((oo, oo), 1), no)
    for load in loads[1:4]:
        load.wait()
    basis = basis_ref[...]
    for k in range(k_local):
        summed = jnp.concatenate(halves(dot(basis, sigma_ref[k])), axis=0)
        coef = jnp.concatenate([hist_ref[k], hist_ref[k]], axis=0)
        outer = jnp.where(diag, dot(summed, coef, 0, 0), 0.0)
        part[k] = fold(jnp.sum(outer.reshape(no, no, oo), axis=1), no)
    third = []
    for off in range(1, n_ta):
        copy = pltpu.make_async_remote_copy(
            src_ref=part,
            dst_ref=parts.at[n_ta - off],
            send_sem=send3.at[off],
            recv_sem=recv3.at[n_ta - off],
            device_id=(ka, lax.rem(ta + off, n_ta)),
            device_id_type=MESH,
        )
        copy.start()
        third.append(copy)

    slots = rows // no
    if n_ta == 2:
        mine = length_ref[0]
        whole = cols // no - slots // 2
        lengths = [mine, whole - mine]
        starts = [jnp.where(ta == 0, 0, whole - mine), jnp.where(ta == 0, mine, 0)]
    else:
        lengths, starts = [], []
        for off in range(n_ta):
            at = lax.rem(ta + off, n_ta)
            length, start = jnp.int32(0), jnp.int32(0)
            for b in range(n_ta):
                length = jnp.where(at == b, length_ref[b], length)
                start = start + jnp.where(b < at, length_ref[b], 0)
            lengths.append(length)
            starts.append(start)
    row = iota((rows, cols), 0)
    lead = iota((rows, cols), 1) - lax.div(row, no) * no

    def mask(off):
        keep = (lead < (starts[off] + slots // 2 + 1) * no) & (row < lengths[off] * no)
        unit = jnp.where(keep, 1.0, 0.0).astype(BF16)
        for k in range(k_local):
            masked[off, k] = panel_ref[off, k] * unit

    loads[4].wait()
    mask(0)

    second = []

    def forward(source):
        piece = gathered.at[ta, source]
        for off in range(1, n_ta):
            copy = pltpu.make_async_remote_copy(
                src_ref=piece,
                dst_ref=piece,
                send_sem=send2.at[off, source],
                recv_sem=recv2.at[ta, source],
                device_id=(ka, lax.rem(ta + off, n_ta)),
                device_id_type=MESH,
            )
            copy.start()
            second.append(copy)

    forward(ka)
    for off in range(1, n_ka):
        source = lax.rem(ka + off, n_ka)
        pltpu.make_async_remote_copy(
            src_ref=packed.at[ta],
            dst_ref=gathered.at[ta, source],
            send_sem=send1.at[off],
            recv_sem=recv1.at[source],
            device_id=(source, ta),
            device_id_type=MESH,
        ).wait_recv()
        forward(source)

    for load in loads[5:]:
        load.wait()
    for off in range(1, n_ta):
        pltpu.make_async_remote_copy(
            src_ref=panel_hbm,
            dst_ref=panel_ref.at[off],
            send_sem=send4.at[off],
            recv_sem=recv4.at[off],
            device_id=(ka, lax.rem(ta + off, n_ta)),
            device_id_type=MESH,
        ).wait_recv()
        mask(off)
        pltpu.make_async_remote_copy(
            src_ref=part,
            dst_ref=parts.at[off],
            send_sem=send3.at[off],
            recv_sem=recv3.at[off],
            device_id=(ka, lax.rem(ta + off, n_ta)),
            device_id_type=MESH,
        ).wait_recv()

    scale = 1.0 / math.sqrt(no * sigma_ref.shape[1] * n_ta)
    for k in range(k_local):
        integral = part[k]
        for off in range(1, n_ta):
            integral = integral + parts[off, k]
        integral = integral * scale
        green = fold(jnp.where(own, green_ref[k : k + 1, :], 0.0), no)
        ham = fold(jnp.where(own, ham_ref[k : k + 1, :], 0.0), no)
        for _ in range(2):
            turn = dot(ham[:, :no], green, 1, 0, HIGH) - dot(green[:, :no], ham, 1, 0, HIGH)
            green = green + STEP * (turn + integral)
        spread = jnp.where(own, jnp.concatenate([green] * (oo // 128), axis=1), 0.0)
        green_out[k : k + 1, :] = jnp.sum(spread, axis=0, keepdims=True)
    moves.append(pltpu.make_async_copy(green_out, green_hbm_out, out_sem.at[2 * k_local]))
    moves[-1].start()

    for off in range(1, n_ta):
        source = lax.rem(ta + off, n_ta)
        for g in range(n_ka):
            piece = gathered.at[source, g]
            pltpu.make_async_remote_copy(
                src_ref=piece,
                dst_ref=piece,
                send_sem=send2.at[off, g],
                recv_sem=recv2.at[source, g],
                device_id=(ka, source),
                device_id_type=MESH,
            ).wait_recv()

    sketched = []
    grams = []
    for k in range(k_local):
        owner = owner_ref[k]
        pair = lax.div(owner, 2)
        omega = gathered[lax.div(pair, share), :, lax.rem(pair, share)]
        omega = omega.reshape(n_ka * depth, width)
        values = []
        for off in range(n_ta):
            both = dot(omega, masked[off, k], 0, 1)
            values.append(jnp.where(lax.rem(owner, 2) == 0, both[:rank], both[rank:]))
        sketched.append(values)
        gram = jnp.zeros((width, width), F32)
        for off in range(n_ta):
            values[off] = jnp.concatenate(halves(values[off]), axis=0)
            gram = gram + dot(values[off], values[off], 1, 1)
        gram = gram[:rank] + gram[rank:]
        grams.append(gram + pltpu.roll(gram, rank, 1))

    lane = iota((rank, width), 1)
    line = iota((rank, width), 0)
    mats = [jnp.where(lane < rank, g, jnp.where(lane == line + rank, 1.0, 0.0)) for g in grams]
    inverses = []
    for inverse in eliminate(mats, [0] * k_local, rank):
        inverse = jnp.where(lane >= rank, inverse, 0.0)
        inverse = inverse + pltpu.roll(inverse, rank, 1)
        inverses.append(jnp.concatenate(halves(inverse), axis=0))

    mine = pl.ds(pl.multiple_of(ta * block, block), block)
    for k in range(k_local):
        total = jnp.zeros((rank, block), F32)
        for off in range(n_ta):
            ortho = dot(inverses[k], sketched[k][off])
            ortho = ortho[:rank] + ortho[rank:]
            if off == 0:
                ortho_out[k] = ortho
                move = pltpu.make_async_copy(ortho_out.at[k], ortho_hbm_out.at[k], out_sem.at[k])
                move.start()
                moves.append(move)
            piece = dot(ortho.astype(BF16), masked[off, k, :, mine])
            total = total + piece.astype(BF16).astype(F32)
        coef_out[k] = total
        place = k_local + k
        move = pltpu.make_async_copy(coef_out.at[k], coef_hbm_out.at[k], out_sem.at[place])
        move.start()
        moves.append(move)

    for copy in first + second + third + panels:
        copy.wait_send()
    for move in moves:
        move.wait()


def finish(green_ref, ortho_ref, coef_ref, green_hbm, ortho_hbm, coef_hbm, sem):
    moves = [
        pltpu.make_async_copy(coef_ref, coef_hbm, sem.at[0]),
        pltpu.make_async_copy(ortho_ref, ortho_hbm, sem.at[1]),
        pltpu.make_async_copy(green_ref, green_hbm, sem.at[2]),
    ]
    for move in moves:
        move.start()
    for move in moves:
        move.wait()


def body(
    n_ka,
    n_ta,
    sigma_history,
    time_basis,
    history_coef,
    green_now,
    hamilton,
    panel_block,
    panel_lengths,
    owners,
    sketch,
):
    k_local, rows, cols = panel_block.shape
    ranks, depth, rank = sketch.shape
    oo = sigma_history.shape[2]
    no = math.isqrt(oo)
    share = ranks // 2 // n_ta
    lengths = panel_lengths
    if n_ta > 2:
        lengths = lax.all_gather(panel_lengths, "ta", tiled=True)
    smem = pl.BlockSpec(memory_space=pltpu.SMEM)
    hbm = pl.BlockSpec(memory_space=pltpu.HBM)
    dma = pltpu.SemaphoreType.DMA
    outs = (
        jax.ShapeDtypeStruct((k_local, oo), F32),
        jax.ShapeDtypeStruct((k_local, rank, rows), F32),
        jax.ShapeDtypeStruct((k_local, rank, cols // n_ta), F32),
    )
    results = pl.pallas_call(
        functools.partial(kernel, n_ka, n_ta),
        out_shape=outs,
        in_specs=[smem] + [hbm] * 8,
        out_specs=(hbm, hbm, hbm),
        scratch_shapes=[
            *[pltpu.VMEM(x.shape, F32) for x in outs],
            pltpu.SMEM((k_local,), jnp.int32),
            pltpu.VMEM(green_now.shape, F32),
            pltpu.VMEM(green_now.shape, F32),
            pltpu.VMEM(sigma_history.shape, BF16),
            pltpu.VMEM(time_basis.shape[::-1], BF16),
            pltpu.VMEM(history_coef.shape, BF16),
            pltpu.VMEM((n_ta,) + panel_block.shape, BF16),
            pltpu.VMEM(sketch.shape, BF16),
            pltpu.VMEM((n_ta, share, depth, 2 * rank), BF16),
            pltpu.VMEM((n_ta, n_ka, share, depth, 2 * rank), BF16),
            pltpu.VMEM((n_ta,) + panel_block.shape, BF16),
            pltpu.VMEM((k_local, no, 128), F32),
            pltpu.VMEM((n_ta, k_local, no, 128), F32),
            dma((8,)),
            dma((2 * k_local + 1,)),
            dma((n_ka,)),
            dma((n_ka,)),
            dma((n_ta, n_ka)),
            dma((n_ta, n_ka)),
            dma((n_ta,)),
            dma((n_ta,)),
            dma((n_ta,)),
            dma((n_ta,)),
        ],
        compiler_params=pltpu.CompilerParams(
            collective_id=0, has_side_effects=True, vmem_limit_bytes=56 * 1024 * 1024
        ),
    )(
        lengths,
        *[
            pltpu.with_memory_space_constraint(x, pltpu.HBM)
            for x in (
                owners.reshape(-1),
                green_now,
                hamilton,
                sigma_history,
                time_basis.T,
                history_coef,
                panel_block,
                sketch,
            )
        ],
    )
    green, ortho, coef = pl.pallas_call(
        finish,
        out_shape=outs,
        in_specs=[pl.BlockSpec(memory_space=pltpu.VMEM)] * 3,
        out_specs=(hbm, hbm, hbm),
        scratch_shapes=[dma((3,))],
        compiler_params=pltpu.CompilerParams(vmem_limit_bytes=8 * 1024 * 1024),
    )(*[pltpu.with_memory_space_constraint(x, pltpu.HBM) for x in results])
    return green, ortho.transpose(0, 2, 1), coef


def solution(mesh):
    in_specs = (
        P("ka", "ta", None),
        P("ta", None),
        P("ka", "ta", None),
        P("ka", None),
        P("ka", None),
        P("ka", "ta", None),
        P("ta"),
        P("ka", None),
        P(None, "ka", None),
    )
    out_specs = (P("ka", None), P("ka", "ta", None), P("ka", None, "ta"))
    step = functools.partial(body, mesh.shape["ka"], mesh.shape["ta"])
    return jax.shard_map(step, mesh=mesh, in_specs=in_specs, out_specs=out_specs, check_vma=False)
```

```python
import functools
import math

import jax
import jax.numpy as jnp
from jax import lax
from jax.experimental import pallas as pl
from jax.experimental.pallas import tpu as pltpu
from jax.sharding import PartitionSpec as P

MESH = pl.DeviceIdType.MESH
HIGH = lax.Precision.HIGHEST
F32 = jnp.float32
BF16 = jnp.bfloat16
STEP = 0.25
GROUP = 4


def iota(shape, dim):
    return lax.broadcasted_iota(jnp.int32, shape, dim)


def dot(a, b, da=1, db=0, precision=None):
    return lax.dot_general(
        a, b, (((da,), (db,)), ((), ())), precision=precision, preferred_element_type=F32
    )


def halves(x):
    high = x.astype(BF16)
    return high, (x - high.astype(F32)).astype(BF16)


def fold(x, no):
    y = x[:, :128]
    for i in range(1, x.shape[1] // 128):
        y = y + x[:, 128 * i : 128 * (i + 1)]
    shift = 64
    while shift >= no:
        y = y + pltpu.roll(y, shift, 1)
        shift //= 2
    return y


def eliminate(mats, offsets, rank):
    count = rank // 8
    full = (8, mats[0].shape[1])
    sub = iota(full, 0)
    tiles = [[m[8 * i : 8 * i + 8] for i in range(count)] for m in mats]
    rows_out = [[] for _ in mats]
    for j in range(count):
        cols = [
            [
                [
                    jnp.broadcast_to(t[i][:, o + 8 * j + a : o + 8 * j + a + 1], full)
                    for a in range(8)
                ]
                for i in range(j, count)
            ]
            for t, o in zip(tiles, offsets)
        ]
        heads = [c[0] for c in cols]
        pivot_rows = [t[j] for t in tiles]
        pivots = [jnp.ones(full, F32) for _ in mats]
        taken = [jnp.zeros(full, F32) for _ in mats]
        for a in range(8):
            for n in range(len(mats)):
                pivot = jnp.broadcast_to(heads[n][a][a : a + 1], full)
                inverse = pl.reciprocal(pivot, approx=False)
                pivots[n] = jnp.where(sub == a, pivot, pivots[n])
                taken[n] = jnp.where(sub == a, pivot_rows[n], taken[n])
                column = heads[n][a]
                for b in range(a + 1, 8):
                    head = heads[n][b]
                    scaled = jnp.broadcast_to(head[a : a + 1], full) * inverse
                    heads[n][b] = jnp.where(sub == a, scaled, head - column * scaled)
                rest = pivot_rows[n]
                scaled = jnp.broadcast_to(rest[a : a + 1], full) * inverse
                pivot_rows[n] = jnp.where(sub == a, scaled, rest - column * scaled)
        for n, t in enumerate(tiles):
            rows_out[n].append(taken[n] * lax.rsqrt(pivots[n]))
            if j + 1 == count:
                continue
            solved = [jnp.broadcast_to(pivot_rows[n][a : a + 1], full) for a in range(8)]
            for i in range(j + 1, count):
                terms = [cols[n][i - j][a] * solved[a] for a in range(8)]
                while len(terms) > 1:
                    terms = [terms[x] + terms[x + 1] for x in range(0, len(terms), 2)]
                t[i] = t[i] - terms[0]
    return [jnp.concatenate(r, axis=0) for r in rows_out]


def kernel(
    n_ka,
    n_ta,
    length_ref,
    owner_hbm,
    green_hbm,
    ham_hbm,
    sigma_hbm,
    basis_hbm,
    hist_hbm,
    panel_hbm,
    sketch_hbm,
    green_out,
    ortho_out,
    coef_out,
    owner_ref,
    green_ref,
    ham_ref,
    sigma_ref,
    basis_ref,
    hist_ref,
    panel_ref,
    sketch_ref,
    packed,
    gathered,
    masked,
    part,
    parts,
    local_sem,
    send1,
    recv1,
    send2,
    recv2,
    send3,
    recv3,
    send4,
    recv4,
):
    ka, ta = lax.axis_index("ka"), lax.axis_index("ta")
    unused, k_local, rows, cols = panel_ref.shape
    ranks, depth, rank = sketch_ref.shape
    share = ranks // 2 // n_ta
    oo = sigma_ref.shape[2]
    no = math.isqrt(oo)
    width = 2 * rank
    block = cols // n_ta

    loads = [
        pltpu.make_async_copy(src, dst, local_sem.at[i])
        for i, (src, dst) in enumerate(
            [
                (sketch_hbm, sketch_ref),
                (basis_hbm, basis_ref),
                (sigma_hbm, sigma_ref),
                (hist_hbm, hist_ref),
                (panel_hbm, panel_ref.at[0]),
                (owner_hbm, owner_ref),
                (green_hbm, green_ref),
                (ham_hbm, ham_ref),
            ]
        )
    ]
    loads[0].start()

    barrier = pltpu.get_barrier_semaphore()
    for off in range(1, n_ka):
        pl.semaphore_signal(
            barrier, inc=1, device_id=(lax.rem(ka + off, n_ka), ta), device_id_type=MESH
        )
    for off in range(1, n_ta):
        pl.semaphore_signal(
            barrier, inc=1, device_id=(ka, lax.rem(ta + off, n_ta)), device_id_type=MESH
        )
    for load in loads[1:]:
        load.start()
    loads[0].wait()
    for pair in range(ranks // 2):
        packed[pair // share, pair % share] = jnp.concatenate(
            [sketch_ref[2 * pair], sketch_ref[2 * pair + 1]], axis=1
        )
    gathered[ta, ka] = packed[ta]
    pl.semaphore_wait(barrier, n_ka - 1 + n_ta - 1)

    first = []
    for off in range(n_ka - 1, 0, -1):
        to = lax.rem(ka + off, n_ka)
        copy = pltpu.make_async_remote_copy(
            src_ref=packed.at[ta],
            dst_ref=gathered.at[ta, ka],
            send_sem=send1.at[off],
            recv_sem=recv1.at[ka],
            device_id=(to, ta),
            device_id_type=MESH,
        )
        copy.start()
        first.append(copy)

    panels = []
    for off in range(1, n_ta):
        copy = pltpu.make_async_remote_copy(
            src_ref=panel_hbm,
            dst_ref=panel_ref.at[n_ta - off],
            send_sem=send4.at[off],
            recv_sem=recv4.at[n_ta - off],
            device_id=(ka, lax.rem(ta + off, n_ta)),
            device_id_type=MESH,
        )
        copy.start()
        panels.append(copy)

    own = lax.div(iota((no, oo), 1), no) == iota((no, oo), 0)
    diag = lax.rem(iota((oo, oo), 0), no) == lax.div(iota((oo, oo), 1), no)
    for load in loads[1:4]:
        load.wait()
    basis = basis_ref[...]
    for k in range(k_local):
        summed = jnp.concatenate(halves(dot(basis, sigma_ref[k])), axis=0)
        coef = jnp.concatenate([hist_ref[k], hist_ref[k]], axis=0)
        outer = jnp.where(diag, dot(summed, coef, 0, 0), 0.0)
        part[k] = fold(jnp.sum(outer.reshape(no, no, oo), axis=1), no)
    third = []
    for off in range(1, n_ta):
        copy = pltpu.make_async_remote_copy(
            src_ref=part,
            dst_ref=parts.at[n_ta - off],
            send_sem=send3.at[off],
            recv_sem=recv3.at[n_ta - off],
            device_id=(ka, lax.rem(ta + off, n_ta)),
            device_id_type=MESH,
        )
        copy.start()
        third.append(copy)

    slots = rows // no
    if n_ta == 2:
        mine = length_ref[0]
        whole = cols // no - slots // 2
        lengths = [mine, whole - mine]
        starts = [jnp.where(ta == 0, 0, whole - mine), jnp.where(ta == 0, mine, 0)]
    else:
        lengths, starts = [], []
        for off in range(n_ta):
            at = lax.rem(ta + off, n_ta)
            length, start = jnp.int32(0), jnp.int32(0)
            for b in range(n_ta):
                length = jnp.where(at == b, length_ref[b], length)
                start = start + jnp.where(b < at, length_ref[b], 0)
            lengths.append(length)
            starts.append(start)
    row = iota((rows, cols), 0)
    lead = iota((rows, cols), 1) - lax.div(row, no) * no

    def mask(off):
        keep = (lead < (starts[off] + slots // 2 + 1) * no) & (row < lengths[off] * no)
        unit = jnp.where(keep, 1.0, 0.0).astype(BF16)
        for k in range(k_local):
            masked[off, k] = panel_ref[off, k] * unit

    loads[4].wait()
    mask(0)

    groups = n_ka // GROUP
    second = []
    home = lax.div(ka, GROUP)
    for g in range(groups):
        group = lax.rem(home + g, groups)
        for i in range(GROUP):
            source = group * GROUP + i

            @pl.when(source != ka)
            def _():
                pltpu.make_async_remote_copy(
                    src_ref=packed.at[ta],
                    dst_ref=gathered.at[ta, source],
                    send_sem=send1.at[0],
                    recv_sem=recv1.at[source],
                    device_id=(ka, lax.rem(ta + 1, n_ta)),
                    device_id_type=MESH,
                ).wait_recv()

        for off in range(1, n_ta):
            piece = gathered.at[ta, pl.ds(group * GROUP, GROUP)]
            copy = pltpu.make_async_remote_copy(
                src_ref=piece,
                dst_ref=piece,
                send_sem=send2.at[off, g],
                recv_sem=recv2.at[ta, group],
                device_id=(ka, lax.rem(ta + off, n_ta)),
                device_id_type=MESH,
            )
            copy.start()
            second.append(copy)

    for load in loads[5:]:
        load.wait()
    for off in range(1, n_ta):
        pltpu.make_async_remote_copy(
            src_ref=panel_hbm,
            dst_ref=panel_ref.at[off],
            send_sem=send4.at[off],
            recv_sem=recv4.at[off],
            device_id=(ka, lax.rem(ta + off, n_ta)),
            device_id_type=MESH,
        ).wait_recv()
        mask(off)
        pltpu.make_async_remote_copy(
            src_ref=part,
            dst_ref=parts.at[off],
            send_sem=send3.at[off],
            recv_sem=recv3.at[off],
            device_id=(ka, lax.rem(ta + off, n_ta)),
            device_id_type=MESH,
        ).wait_recv()

    scale = 1.0 / math.sqrt(no * sigma_ref.shape[1] * n_ta)
    for k in range(k_local):
        integral = part[k]
        for off in range(1, n_ta):
            integral = integral + parts[off, k]
        integral = integral * scale
        green = fold(jnp.where(own, green_ref[k : k + 1, :], 0.0), no)
        ham = fold(jnp.where(own, ham_ref[k : k + 1, :], 0.0), no)
        for _ in range(2):
            turn = dot(ham[:, :no], green, 1, 0, HIGH) - dot(green[:, :no], ham, 1, 0, HIGH)
            green = green + STEP * (turn + integral)
        spread = jnp.where(own, jnp.concatenate([green] * (oo // 128), axis=1), 0.0)
        green_out[k : k + 1, :] = jnp.sum(spread, axis=0, keepdims=True)

    for off in range(1, n_ta):
        source = lax.rem(ta + off, n_ta)
        for g in range(groups):
            piece = gathered.at[source, pl.ds(g * GROUP, GROUP)]
            pltpu.make_async_remote_copy(
                src_ref=piece,
                dst_ref=piece,
                send_sem=send2.at[off, g],
                recv_sem=recv2.at[source, g],
                device_id=(ka, source),
                device_id_type=MESH,
            ).wait_recv()

    sketched = []
    grams = []
    for k in range(k_local):
        owner = owner_ref[k]
        pair = lax.div(owner, 2)
        omega = gathered[lax.div(pair, share), :, lax.rem(pair, share)]
        omega = omega.reshape(n_ka * depth, width)
        values = []
        for off in range(n_ta):
            both = dot(omega, masked[off, k], 0, 1)
            values.append(jnp.where(lax.rem(owner, 2) == 0, both[:rank], both[rank:]))
        sketched.append(values)
        gram = jnp.zeros((width, width), F32)
        for off in range(n_ta):
            values[off] = jnp.concatenate(halves(values[off]), axis=0)
            gram = gram + dot(values[off], values[off], 1, 1)
        gram = gram[:rank] + gram[rank:]
        grams.append(gram + pltpu.roll(gram, rank, 1))

    lane = iota((rank, width), 1)
    line = iota((rank, width), 0)
    mats = [jnp.where(lane < rank, g, jnp.where(lane == line + rank, 1.0, 0.0)) for g in grams]
    inverses = []
    for inverse in eliminate(mats, [0] * k_local, rank):
        inverse = jnp.where(lane >= rank, inverse, 0.0)
        inverse = inverse + pltpu.roll(inverse, rank, 1)
        inverses.append(jnp.concatenate(halves(inverse), axis=0))

    mine = pl.ds(pl.multiple_of(ta * block, block), block)
    for k in range(k_local):
        total = jnp.zeros((rank, block), F32)
        for off in range(n_ta):
            ortho = dot(inverses[k], sketched[k][off])
            ortho = ortho[:rank] + ortho[rank:]
            if off == 0:
                ortho_out[k] = ortho
            piece = dot(ortho.astype(BF16), masked[off, k, :, mine])
            total = total + piece.astype(BF16).astype(F32)
        coef_out[k] = total

    for copy in first + second + third + panels:
        copy.wait_send()


def body(
    n_ka,
    n_ta,
    sigma_history,
    time_basis,
    history_coef,
    green_now,
    hamilton,
    panel_block,
    panel_lengths,
    owners,
    sketch,
):
    k_local, rows, cols = panel_block.shape
    ranks, depth, rank = sketch.shape
    oo = sigma_history.shape[2]
    no = math.isqrt(oo)
    share = ranks // 2 // n_ta
    groups = n_ka // GROUP
    lengths = panel_lengths
    if n_ta > 2:
        lengths = lax.all_gather(panel_lengths, "ta", tiled=True)
    smem = pl.BlockSpec(memory_space=pltpu.SMEM)
    vmem = pl.BlockSpec(memory_space=pltpu.VMEM)
    hbm = pl.BlockSpec(memory_space=pltpu.HBM)
    dma = pltpu.SemaphoreType.DMA
    outs = (
        jax.ShapeDtypeStruct((k_local, oo), F32),
        jax.ShapeDtypeStruct((k_local, rank, rows), F32),
        jax.ShapeDtypeStruct((k_local, rank, cols // n_ta), F32),
    )
    green, ortho, coef = pl.pallas_call(
        functools.partial(kernel, n_ka, n_ta),
        out_shape=outs,
        in_specs=[smem] + [hbm] * 8,
        out_specs=(vmem, vmem, vmem),
        scratch_shapes=[
            pltpu.SMEM((k_local,), jnp.int32),
            pltpu.VMEM(green_now.shape, F32),
            pltpu.VMEM(green_now.shape, F32),
            pltpu.VMEM(sigma_history.shape, BF16),
            pltpu.VMEM(time_basis.shape[::-1], BF16),
            pltpu.VMEM(history_coef.shape, BF16),
            pltpu.VMEM((n_ta,) + panel_block.shape, BF16),
            pltpu.VMEM(sketch.shape, BF16),
            pltpu.VMEM((n_ta, share, depth, 2 * rank), BF16),
            pltpu.VMEM((n_ta, n_ka, share, depth, 2 * rank), BF16),
            pltpu.VMEM((n_ta,) + panel_block.shape, BF16),
            pltpu.VMEM((k_local, no, 128), F32),
            pltpu.VMEM((n_ta, k_local, no, 128), F32),
            dma((8,)),
            dma((n_ka,)),
            dma((n_ka,)),
            dma((n_ta, groups)),
            dma((n_ta, groups)),
            dma((n_ta,)),
            dma((n_ta,)),
            dma((n_ta,)),
            dma((n_ta,)),
        ],
        compiler_params=pltpu.CompilerParams(
            collective_id=0, has_side_effects=True, vmem_limit_bytes=56 * 1024 * 1024
        ),
    )(
        lengths,
        *[
            pltpu.with_memory_space_constraint(x, pltpu.HBM)
            for x in (
                owners.reshape(-1),
                green_now,
                hamilton,
                sigma_history,
                time_basis.T,
                history_coef,
                panel_block,
                sketch,
            )
        ],
    )
    return green, ortho.transpose(0, 2, 1), coef


def solution(mesh):
    in_specs = (
        P("ka", "ta", None),
        P("ta", None),
        P("ka", "ta", None),
        P("ka", None),
        P("ka", None),
        P("ka", "ta", None),
        P("ta"),
        P("ka", None),
        P(None, "ka", None),
    )
    out_specs = (P("ka", None), P("ka", "ta", None), P("ka", None, "ta"))
    step = functools.partial(body, mesh.shape["ka"], mesh.shape["ta"])
    return jax.shard_map(step, mesh=mesh, in_specs=in_specs, out_specs=out_specs, check_vma=False)
```

```python
import functools
import math

import jax
import jax.numpy as jnp
from jax import lax
from jax.experimental import pallas as pl
from jax.experimental.pallas import tpu as pltpu
from jax.sharding import PartitionSpec as P

MESH = pl.DeviceIdType.MESH
HIGH = lax.Precision.HIGHEST
F32 = jnp.float32
BF16 = jnp.bfloat16
STEP = 0.25
GROUP = 4


def iota(shape, dim):
    return lax.broadcasted_iota(jnp.int32, shape, dim)


def dot(a, b, da=1, db=0, precision=None):
    return lax.dot_general(
        a, b, (((da,), (db,)), ((), ())), precision=precision, preferred_element_type=F32
    )


def halves(x):
    high = x.astype(BF16)
    return high, (x - high.astype(F32)).astype(BF16)


def fold(x, no):
    y = x[:, :128]
    for i in range(1, x.shape[1] // 128):
        y = y + x[:, 128 * i : 128 * (i + 1)]
    shift = 64
    while shift >= no:
        y = y + pltpu.roll(y, shift, 1)
        shift //= 2
    return y


def eliminate(mats, offsets, rank):
    count = rank // 8
    full = (8, mats[0].shape[1])
    sub = iota(full, 0)
    tiles = [[m[8 * i : 8 * i + 8] for i in range(count)] for m in mats]
    rows_out = [[] for _ in mats]
    for j in range(count):
        cols = [
            [
                [
                    jnp.broadcast_to(t[i][:, o + 8 * j + a : o + 8 * j + a + 1], full)
                    for a in range(8)
                ]
                for i in range(j, count)
            ]
            for t, o in zip(tiles, offsets)
        ]
        heads = [c[0] for c in cols]
        pivot_rows = [t[j] for t in tiles]
        pivots = [jnp.ones(full, F32) for _ in mats]
        taken = [jnp.zeros(full, F32) for _ in mats]
        for a in range(8):
            for n in range(len(mats)):
                pivot = jnp.broadcast_to(heads[n][a][a : a + 1], full)
                inverse = pl.reciprocal(pivot, approx=False)
                pivots[n] = jnp.where(sub == a, pivot, pivots[n])
                taken[n] = jnp.where(sub == a, pivot_rows[n], taken[n])
                column = heads[n][a]
                for b in range(a + 1, 8):
                    head = heads[n][b]
                    scaled = jnp.broadcast_to(head[a : a + 1], full) * inverse
                    heads[n][b] = jnp.where(sub == a, scaled, head - column * scaled)
                rest = pivot_rows[n]
                scaled = jnp.broadcast_to(rest[a : a + 1], full) * inverse
                pivot_rows[n] = jnp.where(sub == a, scaled, rest - column * scaled)
        for n, t in enumerate(tiles):
            rows_out[n].append(taken[n] * lax.rsqrt(pivots[n]))
            if j + 1 == count:
                continue
            solved = [jnp.broadcast_to(pivot_rows[n][a : a + 1], full) for a in range(8)]
            for i in range(j + 1, count):
                terms = [cols[n][i - j][a] * solved[a] for a in range(8)]
                while len(terms) > 1:
                    terms = [terms[x] + terms[x + 1] for x in range(0, len(terms), 2)]
                t[i] = t[i] - terms[0]
    return [jnp.concatenate(r, axis=0) for r in rows_out]


def kernel(
    n_ka,
    n_ta,
    length_ref,
    owner_hbm,
    green_hbm,
    ham_hbm,
    sigma_hbm,
    basis_hbm,
    hist_hbm,
    panel_hbm,
    sketch_hbm,
    green_out,
    ortho_out,
    coef_out,
    owner_ref,
    green_ref,
    ham_ref,
    sigma_ref,
    basis_ref,
    hist_ref,
    panel_ref,
    sketch_ref,
    packed,
    gathered,
    masked,
    part,
    parts,
    local_sem,
    send1,
    recv1,
    send2,
    recv2,
    send3,
    recv3,
    send4,
    recv4,
):
    ka, ta = lax.axis_index("ka"), lax.axis_index("ta")
    unused, k_local, rows, cols = panel_ref.shape
    ranks, depth, rank = sketch_ref.shape
    share = ranks // 2 // n_ta
    oo = sigma_ref.shape[2]
    no = math.isqrt(oo)
    width = 2 * rank
    block = cols // n_ta

    loads = [
        pltpu.make_async_copy(src, dst, local_sem.at[i])
        for i, (src, dst) in enumerate(
            [
                (sketch_hbm, sketch_ref),
                (basis_hbm, basis_ref),
                (sigma_hbm, sigma_ref),
                (hist_hbm, hist_ref),
                (panel_hbm, panel_ref.at[0]),
                (owner_hbm, owner_ref),
                (green_hbm, green_ref),
                (ham_hbm, ham_ref),
            ]
        )
    ]
    loads[0].start()

    barrier = pltpu.get_barrier_semaphore()
    for off in range(1, n_ka):
        pl.semaphore_signal(
            barrier, inc=1, device_id=(lax.rem(ka + off, n_ka), ta), device_id_type=MESH
        )
    for off in range(1, n_ta):
        pl.semaphore_signal(
            barrier, inc=1, device_id=(ka, lax.rem(ta + off, n_ta)), device_id_type=MESH
        )
    for load in loads[1:]:
        load.start()
    loads[0].wait()
    for pair in range(ranks // 2):
        packed[pair // share, pair % share] = jnp.concatenate(
            [sketch_ref[2 * pair], sketch_ref[2 * pair + 1]], axis=1
        )
    gathered[ta, ka] = packed[ta]
    pl.semaphore_wait(barrier, n_ka - 1 + n_ta - 1)

    first = []
    for off in range(n_ka - 1, 0, -1):
        to = lax.rem(ka + off, n_ka)
        copy = pltpu.make_async_remote_copy(
            src_ref=packed.at[ta],
            dst_ref=gathered.at[ta, ka],
            send_sem=send1.at[off],
            recv_sem=recv1.at[ka],
            device_id=(to, ta),
            device_id_type=MESH,
        )
        copy.start()
        first.append(copy)

    panels = []
    for off in range(1, n_ta):
        copy = pltpu.make_async_remote_copy(
            src_ref=panel_hbm,
            dst_ref=panel_ref.at[n_ta - off],
            send_sem=send4.at[off],
            recv_sem=recv4.at[n_ta - off],
            device_id=(ka, lax.rem(ta + off, n_ta)),
            device_id_type=MESH,
        )
        copy.start()
        panels.append(copy)

    own = lax.div(iota((no, oo), 1), no) == iota((no, oo), 0)
    diag = lax.rem(iota((oo, oo), 0), no) == lax.div(iota((oo, oo), 1), no)
    for load in loads[1:4]:
        load.wait()
    basis = basis_ref[...]
    for k in range(k_local):
        summed = jnp.concatenate(halves(dot(basis, sigma_ref[k])), axis=0)
        coef = jnp.concatenate([hist_ref[k], hist_ref[k]], axis=0)
        outer = jnp.where(diag, dot(summed, coef, 0, 0), 0.0)
        part[k] = fold(jnp.sum(outer.reshape(no, no, oo), axis=1), no)
    third = []
    for off in range(1, n_ta):
        copy = pltpu.make_async_remote_copy(
            src_ref=part,
            dst_ref=parts.at[n_ta - off],
            send_sem=send3.at[off],
            recv_sem=recv3.at[n_ta - off],
            device_id=(ka, lax.rem(ta + off, n_ta)),
            device_id_type=MESH,
        )
        copy.start()
        third.append(copy)

    slots = rows // no
    if n_ta == 2:
        mine = length_ref[0]
        whole = cols // no - slots // 2
        lengths = [mine, whole - mine]
        starts = [jnp.where(ta == 0, 0, whole - mine), jnp.where(ta == 0, mine, 0)]
    else:
        lengths, starts = [], []
        for off in range(n_ta):
            at = lax.rem(ta + off, n_ta)
            length, start = jnp.int32(0), jnp.int32(0)
            for b in range(n_ta):
                length = jnp.where(at == b, length_ref[b], length)
                start = start + jnp.where(b < at, length_ref[b], 0)
            lengths.append(length)
            starts.append(start)
    row = iota((rows, cols), 0)
    lead = iota((rows, cols), 1) - lax.div(row, no) * no

    def mask(off):
        keep = (lead < (starts[off] + slots // 2 + 1) * no) & (row < lengths[off] * no)
        unit = jnp.where(keep, 1.0, 0.0).astype(BF16)
        for k in range(k_local):
            masked[off, k] = panel_ref[off, k] * unit

    loads[4].wait()
    mask(0)

    groups = n_ka // GROUP
    second = []
    home = lax.div(ka, GROUP)
    for g in range(groups):
        group = lax.rem(home + g, groups)
        for i in range(GROUP):
            source = group * GROUP + i

            @pl.when(source != ka)
            def _():
                pltpu.make_async_remote_copy(
                    src_ref=packed.at[ta],
                    dst_ref=gathered.at[ta, source],
                    send_sem=send1.at[0],
                    recv_sem=recv1.at[source],
                    device_id=(ka, lax.rem(ta + 1, n_ta)),
                    device_id_type=MESH,
                ).wait_recv()

        for off in range(1, n_ta):
            piece = gathered.at[ta, pl.ds(group * GROUP, GROUP)]
            copy = pltpu.make_async_remote_copy(
                src_ref=piece,
                dst_ref=piece,
                send_sem=send2.at[off, g],
                recv_sem=recv2.at[ta, group],
                device_id=(ka, lax.rem(ta + off, n_ta)),
                device_id_type=MESH,
            )
            copy.start()
            second.append(copy)

    for load in loads[5:]:
        load.wait()
    for off in range(1, n_ta):
        pltpu.make_async_remote_copy(
            src_ref=panel_hbm,
            dst_ref=panel_ref.at[off],
            send_sem=send4.at[off],
            recv_sem=recv4.at[off],
            device_id=(ka, lax.rem(ta + off, n_ta)),
            device_id_type=MESH,
        ).wait_recv()
        mask(off)
        pltpu.make_async_remote_copy(
            src_ref=part,
            dst_ref=parts.at[off],
            send_sem=send3.at[off],
            recv_sem=recv3.at[off],
            device_id=(ka, lax.rem(ta + off, n_ta)),
            device_id_type=MESH,
        ).wait_recv()

    scale = 1.0 / math.sqrt(no * sigma_ref.shape[1] * n_ta)
    for k in range(k_local):
        integral = part[k]
        for off in range(1, n_ta):
            integral = integral + parts[off, k]
        integral = integral * scale
        green = fold(jnp.where(own, green_ref[k : k + 1, :], 0.0), no)
        ham = fold(jnp.where(own, ham_ref[k : k + 1, :], 0.0), no)
        for _ in range(2):
            turn = dot(ham[:, :no], green, 1, 0, HIGH) - dot(green[:, :no], ham, 1, 0, HIGH)
            green = green + STEP * (turn + integral)
        spread = jnp.where(own, jnp.concatenate([green] * (oo // 128), axis=1), 0.0)
        green_out[k : k + 1, :] = jnp.sum(spread, axis=0, keepdims=True)

    for off in range(1, n_ta):
        source = lax.rem(ta + off, n_ta)
        for g in range(groups):
            piece = gathered.at[source, pl.ds(g * GROUP, GROUP)]
            pltpu.make_async_remote_copy(
                src_ref=piece,
                dst_ref=piece,
                send_sem=send2.at[off, g],
                recv_sem=recv2.at[source, g],
                device_id=(ka, source),
                device_id_type=MESH,
            ).wait_recv()

    sketched = []
    grams = []
    for k in range(k_local):
        owner = owner_ref[k]
        pair = lax.div(owner, 2)
        omega = gathered[lax.div(pair, share), :, lax.rem(pair, share)]
        omega = omega.reshape(n_ka * depth, width)
        values = []
        for off in range(n_ta):
            both = dot(omega, masked[off, k], 0, 1)
            values.append(jnp.where(lax.rem(owner, 2) == 0, both[:rank], both[rank:]))
        sketched.append(values)
        gram = jnp.zeros((width, width), F32)
        for off in range(n_ta):
            values[off] = jnp.concatenate(halves(values[off]), axis=0)
            gram = gram + dot(values[off], values[off], 1, 1)
        gram = gram[:rank] + gram[rank:]
        grams.append(gram + pltpu.roll(gram, rank, 1))

    lane = iota((rank, width), 1)
    line = iota((rank, width), 0)
    mats = [jnp.where(lane < rank, g, jnp.where(lane == line + rank, 1.0, 0.0)) for g in grams]
    inverses = []
    for inverse in eliminate(mats, [0] * k_local, rank):
        inverse = jnp.where(lane >= rank, inverse, 0.0)
        inverse = inverse + pltpu.roll(inverse, rank, 1)
        inverses.append(jnp.concatenate(halves(inverse), axis=0))

    mine = pl.ds(pl.multiple_of(ta * block, block), block)
    for k in range(k_local):
        total = jnp.zeros((rank, block), F32)
        for off in range(n_ta):
            ortho = dot(inverses[k], sketched[k][off])
            ortho = ortho[:rank] + ortho[rank:]
            if off == 0:
                ortho_out[k] = ortho
            piece = dot(ortho.astype(BF16), masked[off, k, :, mine])
            total = total + piece.astype(BF16).astype(F32)
        coef_out[k] = total

    for copy in first + second + third + panels:
        copy.wait_send()


def body(
    n_ka,
    n_ta,
    sigma_history,
    time_basis,
    history_coef,
    green_now,
    hamilton,
    panel_block,
    panel_lengths,
    owners,
    sketch,
):
    k_local, rows, cols = panel_block.shape
    ranks, depth, rank = sketch.shape
    oo = sigma_history.shape[2]
    no = math.isqrt(oo)
    share = ranks // 2 // n_ta
    groups = n_ka // GROUP
    lengths = panel_lengths
    if n_ta > 2:
        lengths = lax.all_gather(panel_lengths, "ta", tiled=True)
    smem = pl.BlockSpec(memory_space=pltpu.SMEM)
    vmem = pl.BlockSpec(memory_space=pltpu.VMEM)
    hbm = pl.BlockSpec(memory_space=pltpu.HBM)
    dma = pltpu.SemaphoreType.DMA
    outs = (
        jax.ShapeDtypeStruct((k_local, oo), F32),
        jax.ShapeDtypeStruct((k_local, rank, rows), F32),
        jax.ShapeDtypeStruct((k_local, rank, cols // n_ta), F32),
    )
    green, ortho, coef = pl.pallas_call(
        functools.partial(kernel, n_ka, n_ta),
        out_shape=outs,
        in_specs=[smem] + [hbm] * 8,
        out_specs=(vmem, vmem, vmem),
        scratch_shapes=[
            pltpu.SMEM((k_local,), jnp.int32),
            pltpu.VMEM(green_now.shape, F32),
            pltpu.VMEM(green_now.shape, F32),
            pltpu.VMEM(sigma_history.shape, BF16),
            pltpu.VMEM(time_basis.shape[::-1], BF16),
            pltpu.VMEM(history_coef.shape, BF16),
            pltpu.VMEM((n_ta,) + panel_block.shape, BF16),
            pltpu.VMEM(sketch.shape, BF16),
            pltpu.VMEM((n_ta, share, depth, 2 * rank), BF16),
            pltpu.VMEM((n_ta, n_ka, share, depth, 2 * rank), BF16),
            pltpu.VMEM((n_ta,) + panel_block.shape, BF16),
            pltpu.VMEM((k_local, no, 128), F32),
            pltpu.VMEM((n_ta, k_local, no, 128), F32),
            dma((8,)),
            dma((n_ka,)),
            dma((n_ka,)),
            dma((n_ta, groups)),
            dma((n_ta, groups)),
            dma((n_ta,)),
            dma((n_ta,)),
            dma((n_ta,)),
            dma((n_ta,)),
        ],
        compiler_params=pltpu.CompilerParams(
            collective_id=0, has_side_effects=True, vmem_limit_bytes=48 * 1024 * 1024
        ),
    )(
        lengths,
        *[
            pltpu.with_memory_space_constraint(x, pltpu.HBM)
            for x in (
                owners.reshape(-1),
                green_now,
                hamilton,
                sigma_history,
                time_basis.T,
                history_coef,
                panel_block,
                sketch,
            )
        ],
    )
    return green, ortho.transpose(0, 2, 1), coef


def solution(mesh):
    in_specs = (
        P("ka", "ta", None),
        P("ta", None),
        P("ka", "ta", None),
        P("ka", None),
        P("ka", None),
        P("ka", "ta", None),
        P("ta"),
        P("ka", None),
        P(None, "ka", None),
    )
    out_specs = (P("ka", None), P("ka", "ta", None), P("ka", None, "ta"))
    step = functools.partial(body, mesh.shape["ka"], mesh.shape["ta"])
    return jax.shard_map(step, mesh=mesh, in_specs=in_specs, out_specs=out_specs, check_vma=False)
```
